256 devices in a mesh: ens: 16 (over z_lo, y), grid: 16 (over x, z_hi, core).
Axes of the slice: x: 4, y: 4, z: 8 (z_hi: 2, z_lo: 4; z = z_hi * 4 + z_lo), core: 2. Of those that a mesh axis runs over, the one named last changes fastest.
Arguments:
- entry_latent_embedding: bfloat16 [16, 4096, 1024], P('ens', 'grid'), may hold values from -16 to 16
- q_weight: bfloat16 [1024, 1024], replicated, may hold values from -1 to 1, as said below
- k_weight: bfloat16 [1024, 1024], replicated, may hold values from -1 to 1, as said below
- v_weight: bfloat16 [1024, 1024], replicated, may hold values from -0.1875 to 0.1875
- o_weight: bfloat16 [1024, 1024], replicated, may hold values from -0.1875 to 0.1875
- channel_to_field_map: bfloat16 [100, 1024], replicated, may hold values from -0.1875 to 0.1875
- targets: float32 [100, 4096], P(None, 'grid'), may hold values from -6 to 6
- area_weight: float32 [4096], P('grid'), may hold values from 0.4 to 4.8
- key_blocks: int32 [32, 3], P('grid'), may hold values from 0 to 31, as said below
Outputs:
- grad_hidden: bfloat16 [16, 4096, 1024], P('ens', 'grid')
- mean_loss: float32 [], replicated
The draws below stay inside these ranges and needn't reach their ends.
Inputs may be any that keep to these rules, and one draw needn't show every extreme that they name: `key_blocks`: row b starts with b itself, then 3 - 1 further distinct blocks no more than 2 away from b and inside the grid. `q_weight`: projection scaled by its fan-in. `k_weight`: projection scaled by its fan-in.
All inputs are finite; a program needn't handle non-finite values.
Results may differ from the reference program's by a relative error of at most 0.025.
The reference program's roundings to bfloat16 on the way count: a program that leaves them out, or rounds other values in their place, can miss the bound.
Values may be sent and summed in bfloat16 or wider, within the bound.
A program may use at most 128 MiB of HBM per device.

```python
import math
import jax
import jax.numpy as jnp
from jax import lax

C = 1024
HEADS = 16
V = 100
BLK = 128
HB = 2
NB = 3
TOK_DEV = 256
BLOCKS = 32
POINTS = 4096
MEMBERS = 16


def mixed_projection(key, salt):
    key = jax.random.fold_in(key, salt)
    own_part = jnp.clip(jax.random.normal(key, (C, C), jnp.float32), -5.0, 5.0)
    blend = jnp.sqrt(1.0) * own_part
    return (blend / jnp.sqrt(jnp.float32(C))).astype(jnp.bfloat16)


def draw_q_weight(key, part):
    return mixed_projection(key, 11)


def draw_k_weight(key, part):
    return mixed_projection(key, 13)


def draw_entry_latent_embedding(key, part):
    key = jax.random.fold_in(key, 3)
    first_key = jax.random.fold_in(key, 0)
    latent_embeddings = jnp.clip(jax.random.normal(first_key, (MEMBERS, POINTS, C), jnp.float32), -4.5, 4.5)
    return latent_embeddings.astype(jnp.bfloat16)


def draw_area_weight(key, part):
    key = jax.random.fold_in(key, 7)
    position = (jnp.arange(POINTS) % TOK_DEV).astype(jnp.float32)
    within = position / max(TOK_DEV - 1, 1)
    ramped = 1.0 + 2.0 * within
    rough = jax.random.uniform(key, (POINTS,), jnp.float32, 0.5, 1.5)
    return ramped * rough


def draw_key_blocks(key, part):
    key = jax.random.fold_in(key, 5)
    own_block = jnp.arange(BLOCKS, dtype=jnp.int32)[:, None]
    offsets = jnp.concatenate([jnp.arange(-HB, 0, dtype=jnp.int32), jnp.arange(1, HB + 1, dtype=jnp.int32)])
    candidate = own_block + offsets[None, :]
    valid = (candidate >= 0) & (candidate < BLOCKS)
    ranking = jax.random.randint(key, (BLOCKS, 2 * HB), 0, 4096) * (2 * HB) + jnp.arange(2 * HB, dtype=jnp.int32)[None, :]
    ranking = jnp.where(valid, ranking, ranking + 16777216)
    order = jnp.argsort(ranking, axis=1, stable=True)
    chosen = jnp.take_along_axis(candidate, order[:, :NB - 1], axis=1)
    return jnp.concatenate([own_block, chosen], axis=1).astype(jnp.int32)


def level_of(own_key, shape, pieces, smallest, top_value):
    gain, own = 1.0, jax.random.fold_in(own_key, 6)
    for dim, shards_of in pieces:
        heights = jnp.exp(jax.random.uniform(jax.random.fold_in(own, dim), (shards_of,), jnp.float32, smallest / len(pieces), top_value / len(pieces)))
        gain = gain * jnp.repeat(heights, shape[dim] // shards_of).reshape([-1 if axis == dim else 1 for axis in range(len(shape))])
    return gain


def normal_values(key, extent, deviation, limit, cuts=(), kind=jnp.bfloat16):
    drawn = deviation * jax.random.normal(key, extent, jnp.float32)
    if cuts:
        drawn = drawn * level_of(key, extent, cuts, -0.22, 0.18)
    return jnp.clip(drawn, -limit, limit).astype(kind)


def setup_inputs(seed: int = 0) -> dict:
    key_list = jax.random.split(jax.random.key(seed), 10)
    entry_latent_embedding = draw_entry_latent_embedding(jax.random.fold_in(key_list[9], 71), 0)
    q_weight = draw_q_weight(jax.random.fold_in(key_list[9], 71), 0)
    k_weight = draw_k_weight(jax.random.fold_in(key_list[9], 71), 0)
    v_weight = normal_values(key_list[3], (C, C), C ** -0.5, 0.1875)
    o_weight = normal_values(key_list[4], (C, C), C ** -0.5, 0.1875)
    channel_to_field_map = normal_values(key_list[5], (V, C), C ** -0.5, 0.1875)
    targets = normal_values(key_list[6], (V, POINTS), 1.0, 6.0, ((1, 16),), jnp.float32)
    area_weight = draw_area_weight(jax.random.fold_in(key_list[9], 71), 0)
    key_blocks = draw_key_blocks(jax.random.fold_in(key_list[9], 71), 0)
    return dict(entry_latent_embedding=entry_latent_embedding, q_weight=q_weight, k_weight=k_weight, v_weight=v_weight, o_weight=o_weight, channel_to_field_map=channel_to_field_map, targets=targets, area_weight=area_weight, key_blocks=key_blocks)


SMOOTH = 0.25

def split_heads(blocks):
    return blocks.reshape(blocks.shape[0], blocks.shape[1], HEADS, blocks.shape[2] // HEADS).astype(jnp.float32)

def attend(query_blk, key_blk, value_blk):
    scaling = 1.0 / math.sqrt(query_blk.shape[2] // HEADS)
    scores = jnp.einsum('brhd,bkhd->bhrk', split_heads(query_blk), split_heads(key_blk)) * scaling
    largest = lax.optimization_barrier(jnp.max(scores, axis=-1, keepdims=True))
    exponent = jnp.exp(scores - largest)
    softmax_score_table = exponent / lax.optimization_barrier(jnp.sum(exponent, axis=-1, keepdims=True))
    midpoint_chance_share = lax.optimization_barrier(softmax_score_table.astype(jnp.bfloat16))
    mixture = jnp.einsum('bhrk,bkhd->brhd', midpoint_chance_share.astype(jnp.float32), split_heads(value_blk))
    return (softmax_score_table, midpoint_chance_share, mixture.reshape(query_blk.shape).astype(jnp.bfloat16))

def attend_back(softmax_score_table, midpoint_chance_share, query_blk, key_blk, value_blk, d_mixture):
    scaling = 1.0 / math.sqrt(query_blk.shape[2] // HEADS)
    d_heads = split_heads(d_mixture)
    d_prob = jnp.einsum('brhd,bkhd->bhrk', d_heads, split_heads(value_blk))
    centre = lax.optimization_barrier(jnp.sum(softmax_score_table * d_prob, axis=-1, keepdims=True))
    d_score = lax.optimization_barrier((softmax_score_table * (d_prob - centre) * scaling).astype(jnp.bfloat16)).astype(jnp.float32)
    d_query = jnp.einsum('bhrk,bkhd->brhd', d_score, split_heads(key_blk)).reshape(query_blk.shape).astype(jnp.bfloat16)
    d_key = jnp.einsum('bhrk,brhd->bkhd', d_score, split_heads(query_blk)).reshape(key_blk.shape)
    d_value = jnp.einsum('bhrk,brhd->bkhd', midpoint_chance_share.astype(jnp.float32), d_heads).reshape(value_blk.shape)
    return (d_query, d_key, d_value)

def crps_terms(ensemble, truth, weight):
    values = ensemble.astype(jnp.float32)
    count_members = values.shape[0]
    misfit = values - truth
    misfit_size = jnp.sqrt(misfit * misfit + SMOOTH * SMOOTH)
    pairwise = values[:, None] - values[None, :]
    pair_size = jnp.sqrt(pairwise * pairwise + SMOOTH * SMOOTH)
    score = lax.optimization_barrier(jnp.sum(misfit_size, axis=0)) - lax.optimization_barrier(jnp.sum(pair_size, axis=(0, 1))) / (2.0 * (count_members - 1))
    total = jnp.sum(weight * score)
    gradient = weight * (misfit / misfit_size - lax.optimization_barrier(jnp.sum(pairwise / pair_size, axis=1)) / (count_members - 1))
    return (gradient, total)

def reference(entry_latent_embedding, q_weight, k_weight, v_weight, o_weight, channel_to_field_map, targets, area_weight, key_blocks):

    def project(latent_embeddings, matrix):
        return jnp.dot(latent_embeddings, matrix, preferred_element_type=jnp.float32).astype(jnp.bfloat16)

    def evaluate_primal_path(latent_embeddings):
        asking_token_vectors = project(latent_embeddings, q_weight).reshape(BLOCKS, BLK, C)
        lookup_token_vectors = project(latent_embeddings, k_weight).reshape(BLOCKS, BLK, C)[key_blocks].reshape(BLOCKS, NB * BLK, C)
        content_token_vectors = project(latent_embeddings, v_weight).reshape(BLOCKS, BLK, C)[key_blocks].reshape(BLOCKS, NB * BLK, C)
        softmax_score_table, midpoint_chance_share, mixture = attend(asking_token_vectors, lookup_token_vectors, content_token_vectors)
        processor_result = (latent_embeddings.astype(jnp.float32) + jnp.dot(mixture.reshape(POINTS, C), o_weight, preferred_element_type=jnp.float32)).astype(jnp.bfloat16)
        single_realisation = lax.dot_general(channel_to_field_map, processor_result, (((1,), (1,)), ((), ())), preferred_element_type=jnp.float32).astype(jnp.bfloat16)
        return (asking_token_vectors, lookup_token_vectors, content_token_vectors, softmax_score_table, midpoint_chance_share, single_realisation)
    predicted_fields_set = lax.map(lambda latent_embeddings: evaluate_primal_path(latent_embeddings)[5], entry_latent_embedding)
    field_wise_result = jnp.moveaxis(predicted_fields_set, 1, 0)
    gradients, totals = lax.map(lambda pair_in: crps_terms(pair_in[0], pair_in[1], area_weight), (field_wise_result, targets))
    grad_half = jnp.moveaxis(gradients, 0, 1).astype(jnp.bfloat16)

    def pull_back(grad_part, matrix):
        return lax.dot_general(grad_part, matrix, (((1,), (1,)), ((), ())), preferred_element_type=jnp.float32)

    def pull_exact(grad_part, matrix):
        return lax.dot_general(grad_part, matrix.astype(jnp.float32), (((1,), (1,)), ((), ())), precision=lax.Precision.HIGHEST, preferred_element_type=jnp.float32)

    def backward(inputs):
        latent_embeddings, grad_member = inputs
        asking_token_vectors, lookup_token_vectors, content_token_vectors, softmax_score_table, midpoint_chance_share, single_realisation = evaluate_primal_path(latent_embeddings)
        d_output = lax.dot_general(grad_member, channel_to_field_map, (((0,), (0,)), ((), ())), preferred_element_type=jnp.float32)
        d_mixture = pull_back(d_output.astype(jnp.bfloat16), o_weight).astype(jnp.bfloat16)
        d_query, d_key, d_value = attend_back(softmax_score_table, midpoint_chance_share, asking_token_vectors, lookup_token_vectors, content_token_vectors, d_mixture.reshape(BLOCKS, BLK, C))
        segment_ids = key_blocks.reshape(-1)
        key_sum = jax.ops.segment_sum(d_key.reshape(BLOCKS * NB, BLK, C), segment_ids, num_segments=BLOCKS).reshape(POINTS, C)
        value_sum = jax.ops.segment_sum(d_value.reshape(BLOCKS * NB, BLK, C), segment_ids, num_segments=BLOCKS).reshape(POINTS, C)
        result = d_output + pull_back(d_query.reshape(POINTS, C), q_weight) + pull_exact(key_sum, k_weight) + pull_exact(value_sum, v_weight)
        return result.astype(jnp.bfloat16)
    grad_hidden = lax.map(backward, (entry_latent_embedding, grad_half))
    mean_loss = jnp.sum(totals) / (POINTS * V)
    return (grad_hidden, mean_loss)
```

```python
import functools

import jax
import jax.numpy as jnp
from jax import lax
from jax.experimental import pallas as pl
from jax.experimental.pallas import tpu as pltpu
from jax.sharding import PartitionSpec as P

MESH = pl.DeviceIdType.MESH
SMOOTH = 0.25
BIG = 1e30
NEG = -1e30
F32 = jnp.float32
BF16 = jnp.bfloat16


def nt(a, b):
    return lax.dot_general(a, b, (((1,), (1,)), ((), ())), preferred_element_type=F32)


def nn(a, b):
    return lax.dot_general(a, b, (((1,), (0,)), ((), ())), preferred_element_type=F32)


def heads_of(row):
    return jnp.concatenate(
        [
            jnp.broadcast_to(row[:, :128], (64, 128)),
            jnp.broadcast_to(row[:, 128:], (64, 128)),
        ],
        axis=0,
    )


def diagonal(pair):
    return jnp.concatenate([pair[:64, :128], pair[64:, 128:]], axis=0)


def kernel(
    ne,
    ng,
    kb_ref,
    x_hbm,
    wq_hbm,
    wk_hbm,
    wv_hbm,
    wo_hbm,
    mp_hbm,
    truth_ref,
    weight_ref,
    out_ref,
    loss_ref,
    WQ,
    WK,
    WV,
    WO,
    MP,
    X,
    K,
    V,
    KT,
    VT,
    QQ,
    DD,
    E,
    ACC,
    MS,
    L,
    LSE,
    LO,
    LR,
    MIXF,
    MIXB,
    OUTB,
    FC,
    RV,
    Y,
    G,
    GF,
    PF,
    DO,
    DOB,
    DQ,
    DK,
    DV,
    DKB,
    DVB,
    C,
    CR,
    LS,
    loc,
    xs,
    xr,
    a1s,
    a1r,
    a2s,
    a2r,
    gs,
    gr,
    ls,
    lr,
    cs,
    cr,
    ts,
    tr,
):
    e = lax.axis_index("ens")
    g = lax.axis_index("grid")
    core = lax.rem(g, 2)
    far = g - 1 + 2 * core
    near = g + 1 - 2 * core
    has_far = (far >= 0) & (far < ng)

    def load(src, dst, i):
        return pltpu.make_async_copy(src, dst, loc.at[i])

    lx = [
        load(x_hbm.at[pl.ds(pl.multiple_of(core * 128, 128), 128)], X.at[2], 0),
        load(x_hbm.at[pl.ds(pl.multiple_of((1 - core) * 128, 128), 128)], X.at[3], 1),
    ]
    lk, lv, lq = load(wk_hbm, WK, 2), load(wv_hbm, WV, 3), load(wq_hbm, WQ, 4)
    lo, lm = load(wo_hbm, WO, 5), load(mp_hbm, MP, 6)
    for c in lx + [lk, lv, lq, lo, lm]:
        c.start()

    barrier = pltpu.get_barrier_semaphore()

    @pl.loop(1, ne)
    def _(d):
        pl.semaphore_signal(barrier, inc=1, device_id=(lax.rem(e + d, ne), g), device_id_type=MESH)

    @pl.loop(1, ng)
    def _(d):
        pl.semaphore_signal(barrier, inc=1, device_id=(e, lax.rem(g + d, ng)), device_id_type=MESH)

    @pl.when(jnp.logical_not(has_far))
    def _():
        X[0:2] = jnp.zeros((2, 128, 1024), BF16)
        GF[0:2] = jnp.zeros((2, 128, 128), BF16)
        LR[0] = jnp.full((3, 8, 256), BIG, F32)
        CR[0] = jnp.zeros((2, 8, 256), F32)

    for c in lx:
        c.wait()
    pl.semaphore_wait(barrier, ne - 1 + ng - 1)

    def to(src, dst, s, r, dev):
        return pltpu.make_async_remote_copy(
            src_ref=src, dst_ref=dst, send_sem=s, recv_sem=r, device_id=dev, device_id_type=MESH
        )

    x_far = [to(X.at[2], X.at[1], xs.at[0], xr.at[0], (e, far)), to(X.at[3], X.at[0], xs.at[1], xr.at[1], (e, far))]
    x_near = [to(X.at[3], X.at[4], xs.at[2], xr.at[2], (e, near)), to(X.at[2], X.at[5], xs.at[3], xr.at[3], (e, near))]

    @pl.when(has_far)
    def _():
        for c in x_far:
            c.start()

    for c in x_near:
        c.start()

    def slot_of(block):
        return jnp.where(core == 0, block - (2 * g - 2), 2 * g + 3 - block)

    seen = []
    for q in range(2):
        ids = [jnp.where(core == 0, slot_of(kb_ref[q, n]), slot_of(kb_ref[1 - q, n])) for n in range(3)]
        seen.append([(ids[0] == s) | (ids[1] == s) | (ids[2] == s) for s in range(6)])

    low = lax.broadcasted_iota(jnp.int32, (1, 128), 1) < 64

    def stacked(block):
        zero = jnp.zeros_like(block)
        return jnp.concatenate([jnp.where(low, block, zero), jnp.where(low, zero, block)], axis=0)

    def rows_of(ref, slot, count):
        return ref[slot : slot + count].reshape(count * 128, 1024)

    def project_kv(W, D, DT, slot, count):
        @pl.loop(0, 4)
        def _(j):
            r = nn(rows_of(X, slot, count), W[:, pl.ds(pl.multiple_of(j * 256, 256), 256)]).astype(BF16)
            for h in range(2):
                part = r[:, h * 128 : (h + 1) * 128]
                D[2 * j + h, slot * 128 : (slot + count) * 128, :] = part
                DT[2 * j + h, :, slot * 128 : (slot + count) * 128] = part.T

    def project_q(slot, count):
        @pl.loop(0, 4)
        def _(j):
            r = nn(rows_of(X, slot, count), WQ[:, pl.ds(pl.multiple_of(j * 256, 256), 256)]).astype(BF16)
            r = (r.astype(F32) * 0.125).astype(BF16)
            for h in range(2):
                for i in range(count):
                    QQ[2 * j + h, slot + i] = stacked(r[i * 128 : (i + 1) * 128, h * 128 : (h + 1) * 128])

    def attend(qi, first, last, step, final):
        n = last - first + 1
        off = (first - qi) * 128

        @pl.loop(0, 8)
        def _(hp):
            row = pl.ds(hp, 1)
            s = nt(K[hp, first * 128 : (last + 1) * 128, :], QQ[hp, 2 + qi])
            if step:
                m_old = MS[qi, step - 1, row, :]
                m = m_old
            else:
                m = jnp.full((1, 256), NEG, F32)
            parts = [s[i * 128 : (i + 1) * 128] for i in range(n)]
            for i, part in enumerate(parts):
                m = jnp.maximum(m, jnp.where(seen[qi][first + i], jnp.max(part, axis=0, keepdims=True), NEG))
            total = jnp.zeros((1, 256), F32)
            exps = []
            for i, part in enumerate(parts):
                x = jnp.exp(part - jnp.where(seen[qi][first + i], m, BIG))
                total = total + jnp.sum(x, axis=0, keepdims=True)
                exps.append(x.astype(BF16))
            eb = jnp.concatenate(exps, axis=0) if n > 1 else exps[0]
            E[qi, hp, off : off + n * 128, :] = eb
            acc = diagonal(nn(VT[hp, :, first * 128 : (last + 1) * 128], eb))
            if step:
                alpha = jnp.exp(m_old - m)
                total = total + L[qi, row, :] * alpha
                acc = acc + ACC[qi, hp] * heads_of(alpha)
            MS[qi, step, row, :] = m
            if final:
                LSE[qi, row, :] = m + jnp.log(total)
                mix = (acc * heads_of(1.0 / total)).T
                lanes = pl.ds(pl.multiple_of(hp * 128, 128), 128)
                MIXF[qi, :, lanes] = mix
                MIXB[qi, :, lanes] = mix.astype(BF16)
            else:
                L[qi, row, :] = total
                ACC[qi, hp] = acc

    def decode(qi):
        @pl.loop(0, 4)
        def _(j):
            lanes = pl.ds(pl.multiple_of(j * 256, 256), 256)
            r = X[2 + qi, :, lanes].astype(F32) + nn(MIXB[qi], WO[:, lanes])
            OUTB[qi, :, lanes] = r.astype(BF16)

        FC[qi] = nt(OUTB[qi], MP[...]).astype(BF16)

    def place(t):
        half = t // 8
        return jnp.where(core == 0, half, 1 - half), pl.multiple_of(lax.rem(t, 8) * 16, 16)

    def a1(d):
        t = lax.rem(e + d, ne)
        b, r = place(t)
        return to(FC.at[b, pl.ds(r, 16)], RV.at[e], a1s.at[d], a1r.at[d], (t, g))

    lk.wait()
    lv.wait()
    project_kv(WK, K, KT, 2, 2)
    project_kv(WV, V, VT, 2, 2)
    lq.wait()
    project_q(2, 2)
    for c in x_near:
        c.wait_recv()
    project_kv(WK, K, KT, 4, 2)
    project_kv(WV, V, VT, 4, 2)
    attend(0, 2, 4, 0, False)
    attend(1, 2, 5, 0, False)
    project_q(4, 2)
    lo.wait()
    lm.wait()

    @pl.when(has_far)
    def _():
        x_far[0].wait_recv()

    project_kv(WK, K, KT, 1, 1)
    project_kv(WV, V, VT, 1, 1)
    attend(1, 1, 1, 1, True)
    attend(0, 1, 1, 1, False)
    decode(1)

    @pl.when(has_far)
    def _():
        x_far[1].wait_recv()

    project_kv(WK, K, KT, 0, 1)
    project_kv(WV, V, VT, 0, 1)
    attend(0, 0, 0, 2, True)
    decode(0)

    @pl.loop(1, ne)
    def _(d):
        a1(d).start()

    b_own, r_own = place(e)
    RV[e] = FC[b_own, pl.ds(r_own, 16), :]

    def shown(qi, s):
        return jnp.where(seen[qi][s], LSE[qi], BIG)

    LO[0, 0], LO[0, 1], LO[0, 2] = shown(0, 1), shown(0, 0), shown(1, 1)
    LO[1, 0], LO[1, 1], LO[1, 2] = shown(1, 5), shown(1, 4), shown(0, 4)
    l_far = to(LO.at[0], LR.at[0], ls.at[0], lr.at[0], (e, far))
    l_near = to(LO.at[1], LR.at[1], ls.at[1], lr.at[1], (e, near))

    @pl.when(has_far)
    def _():
        l_far.start()

    l_near.start()

    @pl.loop(0, 8)
    def _(hp):
        row = pl.ds(hp, 1)
        for qi in range(2):
            lse = LSE[qi, row, :]
            spans = ((2, 4), (1, 1), (0, 0)) if qi == 0 else ((2, 5), (1, 1))
            for step, (first, last) in enumerate(spans):
                scale = jnp.exp(MS[qi, step, row, :] - lse)
                a, b = (first - qi) * 128, (last + 1 - qi) * 128
                E[qi, hp, a:b, :] = (E[qi, hp, a:b, :].astype(F32) * scale).astype(BF16)

    project_q(0, 2)

    sides = ((1, 0, 256), (4, 5, 384))

    def foreign(side):
        q1, q2, k2 = sides[side]

        @pl.loop(0, 8)
        def _(hp):
            row = pl.ds(hp, 1)
            s1 = nt(K[hp, 256:512, :], QQ[hp, q1])
            PF[side, hp, 0:128] = jnp.exp(s1[:128] - LR[side, 0, row, :]).astype(BF16)
            PF[side, hp, 128:256] = jnp.exp(s1[128:] - LR[side, 1, row, :]).astype(BF16)
            s2 = nt(K[hp, k2 : k2 + 128, :], QQ[hp, q2])
            PF[side, hp, 256:384] = jnp.exp(s2 - LR[side, 2, row, :]).astype(BF16)

    l_near.wait_recv()
    foreign(1)

    @pl.loop(1, ne)
    def _(d):
        a1(d).wait_recv()

    Y[...] = RV[...].astype(F32)
    truth = truth_ref[...]
    weight = weight_ref[...]

    def score(i, total):
        y = Y[i]
        d = y - truth
        v = d * d + SMOOTH * SMOOTH
        r = lax.rsqrt(v)
        pd = y[None] - Y[...]
        pv = pd * pd + SMOOTH * SMOOTH
        pr = lax.rsqrt(pv)
        grad = weight * (d * r - jnp.sum(pd * pr, axis=0) / (ne - 1))
        G[i] = grad.astype(BF16)
        return total + (v * r - jnp.sum(pv * pr, axis=0) / (2.0 * (ne - 1)))

    total = lax.fori_loop(0, ne, score, jnp.zeros((16, 128), F32))
    partial = jnp.sum(jnp.sum(total * weight, axis=0, keepdims=True), axis=1, keepdims=True)
    p_hi = partial.astype(BF16).astype(F32)
    p_mid = (partial - p_hi).astype(BF16).astype(F32)
    p_lo = partial - p_hi - p_mid
    lane = lax.broadcasted_iota(jnp.int32, (16, 128), 1)
    first_row = lax.broadcasted_iota(jnp.int32, (16, 128), 0) == 0
    rider = jnp.where(lane == 104, p_hi, jnp.where(lane == 105, p_mid, jnp.where(lane == 106, p_lo, 0.0)))
    rider = jnp.where(first_row, rider, 0.0)

    def ride(i, carry):
        G[i] = (G[i].astype(F32) + rider).astype(BF16)
        return carry

    lax.fori_loop(0, ne, ride, 0)

    def a2(d):
        t = lax.rem(e + d, ne)
        b, r = place(e)
        return to(G.at[t], GF.at[2 + b, pl.ds(r, 16)], a2s.at[d], a2r.at[d], (t, g))

    @pl.loop(1, ne)
    def _(d):
        a2(d).start()

    GF[2 + b_own, pl.ds(r_own, 16), :] = G[e]

    @pl.when(has_far)
    def _():
        l_far.wait_recv()

    foreign(0)

    def a2_in(d):
        b, r = place(lax.rem(e - d + ne, ne))
        return to(G.at[0], GF.at[2 + b, pl.ds(r, 16)], a2s.at[d], a2r.at[d], (e, g))

    @pl.loop(1, ne)
    def _(d):
        a2_in(d).wait_recv()

    g_far = [to(GF.at[2], GF.at[1], gs.at[0], gr.at[0], (e, far)), to(GF.at[3], GF.at[0], gs.at[1], gr.at[1], (e, far))]
    g_near = [to(GF.at[3], GF.at[4], gs.at[2], gr.at[2], (e, near)), to(GF.at[2], GF.at[5], gs.at[3], gr.at[3], (e, near))]

    @pl.when(has_far)
    def _():
        for c in g_far:
            c.start()

    for c in g_near:
        c.start()

    mine = GF[2:4].reshape(256, 128).astype(F32)
    lane = lax.broadcasted_iota(jnp.int32, (256, 128), 1)
    mine = jnp.where((lane >= 104) & (lane < 107), mine, 0.0)
    band = jnp.sum(jnp.sum(mine, axis=0, keepdims=True), axis=1, keepdims=True)
    LS[g] = jnp.broadcast_to(band, (8, 128))

    def tell(d):
        return to(LS.at[g], LS.at[g], ts.at[d], tr.at[d], (e, lax.rem(g + d, ng)))

    def told(d):
        s = lax.rem(g - d + ng, ng)
        return to(LS.at[s], LS.at[s], ts.at[d], tr.at[d], (e, g))

    @pl.loop(1, ng)
    def _(d):
        tell(d).start()

    indicator = (lax.broadcasted_iota(jnp.int32, (8, 128), 1) // 64) == lax.broadcasted_iota(jnp.int32, (8, 128), 0)
    indicator = jnp.where(indicator, 1.0, 0.0).astype(BF16)

    def d_mix(slot, count, own):
        @pl.loop(0, 4)
        def _(j):
            lanes = pl.ds(pl.multiple_of(j * 256, 256), 256)
            r = nn(GF[slot : slot + count].reshape(count * 128, 128), MP[:, lanes])
            if own:
                DO[:, lanes] = r
            DOB[slot * 128 : (slot + count) * 128, lanes] = r.astype(BF16)

        @pl.loop(0, 4)
        def _(j):
            lanes = pl.ds(pl.multiple_of(j * 256, 256), 256)
            r = nt(DOB[slot * 128 : (slot + count) * 128, :], WO[lanes, :]).astype(BF16)
            for h in range(2):
                for i in range(count):
                    part = r[i * 128 : (i + 1) * 128, h * 128 : (h + 1) * 128]
                    DD[2 * j + h, slot + i] = stacked(part)
                    if own:
                        hp_lanes = pl.ds(pl.multiple_of(j * 256 + h * 128, 128), 128)
                        prod = part.astype(F32) * MIXF[i, :, hp_lanes]
                        hi = prod.astype(BF16)
                        low_part = (prod - hi.astype(F32)).astype(BF16)
                        c = nt(indicator, hi) + nt(indicator, low_part)
                        C[i, pl.ds(2 * j + h, 1), :] = jnp.concatenate([c[0:1], c[1:2]], axis=1)

    d_mix(2, 2, True)
    c_far = to(C, CR.at[0], cs.at[0], cr.at[0], (e, far))
    c_near = to(C, CR.at[1], cs.at[1], cr.at[1], (e, near))

    @pl.when(has_far)
    def _():
        c_far.start()

    c_near.start()

    @pl.loop(0, 8)
    def _(hp):
        row = pl.ds(hp, 1)
        dk = jnp.zeros((256, 128), F32)
        dv = jnp.zeros((256, 128), F32)
        for qi in range(2):
            span = slice(qi * 128, qi * 128 + 640)
            dp = nt(V[hp, span, :], DD[hp, 2 + qi])
            p = E[qi, hp]
            ds = (p.astype(F32) * (dp - C[qi, row, :])).astype(BF16)
            dq = diagonal(nn(KT[hp, :, span], ds)).T * 0.125
            DQ[qi, :, pl.ds(pl.multiple_of(hp * 128, 128), 128)] = dq.astype(BF16)
            own = slice((2 - qi) * 128, (4 - qi) * 128)
            dk = dk + nn(ds[own], QQ[hp, 2 + qi])
            dv = dv + nn(p[own], DD[hp, 2 + qi])
        DK[hp] = dk
        DV[hp] = dv

    def foreign_back(side, final):
        q1, q2, k2 = sides[side]
        c1, c2 = (0, 1) if side == 0 else (1, 0)

        @pl.loop(0, 8)
        def _(hp):
            row = pl.ds(hp, 1)
            p1 = PF[side, hp, 0:256]
            ds1 = (p1.astype(F32) * (nt(V[hp, 256:512, :], DD[hp, q1]) - CR[side, c1, row, :])).astype(BF16)
            dk = DK[hp] + nn(ds1, QQ[hp, q1])
            dv = DV[hp] + nn(p1, DD[hp, q1])
            p2 = PF[side, hp, 256:384]
            ds2 = (p2.astype(F32) * (nt(V[hp, k2 : k2 + 128, :], DD[hp, q2]) - CR[side, c2, row, :])).astype(BF16)
            dk2 = nn(ds2, QQ[hp, q2])
            dv2 = nn(p2, DD[hp, q2])
            if side == 0:
                dk = jnp.concatenate([dk[:128] + dk2, dk[128:]], axis=0)
                dv = jnp.concatenate([dv[:128] + dv2, dv[128:]], axis=0)
            else:
                dk = jnp.concatenate([dk[:128], dk[128:] + dk2], axis=0)
                dv = jnp.concatenate([dv[:128], dv[128:] + dv2], axis=0)
            if final:
                lanes = pl.ds(pl.multiple_of(hp * 128, 128), 128)
                DKB[:, lanes] = dk.astype(BF16)
                DVB[:, lanes] = dv.astype(BF16)
            else:
                DK[hp] = dk
                DV[hp] = dv

    for c in g_near:
        c.wait_recv()
    d_mix(4, 2, False)
    c_near.wait_recv()
    foreign_back(1, False)

    @pl.loop(0, 4)
    def _(j):
        lanes = pl.ds(pl.multiple_of(j * 256, 256), 256)
        DO[:, lanes] = DO[:, lanes] + nt(DQ[...].reshape(256, 1024), WQ[lanes, :])

    @pl.when(has_far)
    def _():
        for c in g_far:
            c.wait_recv()

    d_mix(0, 2, False)

    @pl.when(has_far)
    def _():
        c_far.wait_recv()

    foreign_back(0, True)

    @pl.loop(0, 4)
    def _(j):
        lanes = pl.ds(pl.multiple_of(j * 256, 256), 256)
        r = (DO[:, lanes] + nt(DKB[...], WK[lanes, :]) + nt(DVB[...], WV[lanes, :])).astype(BF16)
        out_ref[pl.ds(pl.multiple_of(core * 128, 128), 128), lanes] = r[:128]
        out_ref[pl.ds(pl.multiple_of((1 - core) * 128, 128), 128), lanes] = r[128:]

    @pl.loop(1, ng)
    def _(d):
        told(d).wait_recv()

    loss_ref[...] = jnp.sum(LS[...], axis=0)

    @pl.when(has_far)
    def _():
        for c in x_far + g_far + [l_far, c_far]:
            c.wait_send()

    for c in x_near + g_near + [l_near, c_near]:
        c.wait_send()

    @pl.loop(1, ne)
    def _(d):
        a1(d).wait_send()
        a2(d).wait_send()

    @pl.loop(1, ng)
    def _(d):
        tell(d).wait_send()


def shards(x, wq, wk, wv, wo, decoder, targets, area_weight, key_blocks):
    ne, ng = lax.axis_size("ens"), lax.axis_size("grid")
    points, channels = x.shape[1:]
    variables = decoder.shape[0]
    start = lax.axis_index("ens") * (points // ne)
    truth = lax.dynamic_slice_in_dim(targets, start, points // ne, 1).T
    truth = jnp.pad(truth, ((0, 0), (0, 128 - variables)))
    weight = lax.dynamic_slice_in_dim(area_weight, start, points // ne, 0)
    weight = jnp.pad(jnp.broadcast_to(weight[:, None], (points // ne, variables)), ((0, 0), (0, 128 - variables)))
    padded = jnp.pad(decoder, ((0, 128 - variables), (0, 0)))
    vm = pltpu.VMEM
    dma = pltpu.SemaphoreType.DMA
    scratch = [vm((1024, 1024), BF16)] * 4 + [
        vm((128, 1024), BF16),
        vm((6, 128, 1024), BF16),
        vm((8, 768, 128), BF16),
        vm((8, 768, 128), BF16),
        vm((8, 128, 768), BF16),
        vm((8, 128, 768), BF16),
        vm((8, 6, 256, 128), BF16),
        vm((8, 6, 256, 128), BF16),
        vm((2, 8, 640, 256), BF16),
        vm((2, 8, 128, 128), F32),
        vm((2, 3, 8, 256), F32),
        vm((2, 8, 256), F32),
        vm((2, 8, 256), F32),
        vm((2, 3, 8, 256), F32),
        vm((2, 3, 8, 256), F32),
        vm((2, 128, 1024), F32),
        vm((2, 128, 1024), BF16),
        vm((2, 128, 1024), BF16),
        vm((2, 128, 128), BF16),
        vm((16, 16, 128), BF16),
        vm((16, 16, 128), F32),
        vm((16, 16, 128), BF16),
        vm((6, 128, 128), BF16),
        vm((2, 8, 384, 256), BF16),
        vm((256, 1024), F32),
        vm((768, 1024), BF16),
        vm((2, 128, 1024), BF16),
        vm((8, 256, 128), F32),
        vm((8, 256, 128), F32),
        vm((256, 1024), BF16),
        vm((256, 1024), BF16),
        vm((2, 8, 256), F32),
        vm((2, 2, 8, 256), F32),
        vm((16, 8, 128), F32),
        dma((7,)),
        dma((4,)),
        dma((4,)),
        dma((16,)),
        dma((16,)),
        dma((16,)),
        dma((16,)),
        dma((4,)),
        dma((4,)),
        dma((2,)),
        dma((2,)),
        dma((2,)),
        dma((2,)),
        dma((16,)),
        dma((16,)),
    ]
    anywhere = pl.BlockSpec(memory_space=pl.ANY)
    in_vmem = pl.BlockSpec(memory_space=pltpu.VMEM)
    grad, loss = pl.pallas_call(
        functools.partial(kernel, ne, ng),
        out_shape=(
            jax.ShapeDtypeStruct((points, channels), BF16),
            jax.ShapeDtypeStruct((8, 128), F32),
        ),
        in_specs=[pl.BlockSpec(memory_space=pltpu.SMEM)] + [anywhere] * 6 + [in_vmem] * 2,
        out_specs=(in_vmem, in_vmem),
        scratch_shapes=scratch,
        compiler_params=pltpu.CompilerParams(
            collective_id=0, has_side_effects=True, vmem_limit_bytes=58 * 1024 * 1024
        ),
        name="whole",
    )(key_blocks, x[0], wq, wk, wv, wo, padded, truth, weight)
    return grad[None], loss[0, 0] / (points * ng * variables)


def solution(mesh):
    return jax.shard_map(
        shards,
        mesh=mesh,
        in_specs=(
            P("ens", "grid", None),
            P(),
            P(),
            P(),
            P(),
            P(),
            P(None, "grid"),
            P("grid"),
            P("grid", None),
        ),
        out_specs=(P("ens", "grid", None), P()),
        check_vma=False,
    )
```

```python
import functools

import jax
import jax.numpy as jnp
from jax import lax
from jax.experimental import pallas as pl
from jax.experimental.pallas import tpu as pltpu
from jax.sharding import PartitionSpec as P

MESH = pl.DeviceIdType.MESH
SMOOTH = 0.25
BIG = 1e30
NEG = -1e30
F32 = jnp.float32
BF16 = jnp.bfloat16
UNROLL = 8
UNROLL_OWN = 2
UNROLL_BACK = 4


def nt(a, b):
    return lax.dot_general(a, b, (((1,), (1,)), ((), ())), preferred_element_type=F32)


def nn(a, b):
    return lax.dot_general(a, b, (((1,), (0,)), ((), ())), preferred_element_type=F32)


def heads_of(row):
    return jnp.concatenate(
        [
            jnp.broadcast_to(row[:, :128], (64, 128)),
            jnp.broadcast_to(row[:, 128:], (64, 128)),
        ],
        axis=0,
    )


def diagonal(pair):
    return jnp.concatenate([pair[:64, :128], pair[64:, 128:]], axis=0)


def unrolled(count, group, body):
    if group == count:
        for i in range(count):
            body(i)
    else:

        @pl.loop(0, count // group)
        def _(k):
            for i in range(group):
                body(k * group + i)


def span(i, width):
    if isinstance(i, int):
        return slice(i * width, (i + 1) * width)
    return pl.ds(pl.multiple_of(i * width, width), width)


def kernel(
    ne,
    ng,
    variables,
    kb_ref,
    area_ref,
    x_hbm,
    wq_hbm,
    wk_hbm,
    wv_hbm,
    wo_hbm,
    decoder_ref,
    targets_ref,
    out_ref,
    loss_ref,
    WQ,
    WK,
    WV,
    WO,
    MP,
    MW,
    TT,
    X,
    K,
    V,
    KT,
    VT,
    QQ,
    DD,
    E,
    ACC,
    MS,
    L,
    LSE,
    LO,
    LR,
    MIXF,
    MIXB,
    FX,
    FC,
    RV,
    Y,
    G,
    GF,
    PF,
    DO,
    DQ,
    DK,
    DV,
    DKB,
    DVB,
    C,
    CR,
    LS,
    loc,
    xs,
    xr,
    a1s,
    a1r,
    a2s,
    a2r,
    gs,
    gr,
    ls,
    lr,
    cs,
    cr,
    ts,
    tr,
):
    e = lax.axis_index("ens")
    g = lax.axis_index("grid")
    core = lax.rem(g, 2)
    far = g - 1 + 2 * core
    near = g + 1 - 2 * core
    has_far = (far >= 0) & (far < ng)

    def load(src, dst, i):
        return pltpu.make_async_copy(src, dst, loc.at[i])

    lx = [
        load(x_hbm.at[pl.ds(pl.multiple_of(core * 128, 128), 128)], X.at[2], 0),
        load(x_hbm.at[pl.ds(pl.multiple_of((1 - core) * 128, 128), 128)], X.at[3], 1),
    ]
    lk, lv, lq = load(wk_hbm, WK, 2), load(wv_hbm, WV, 3), load(wq_hbm, WQ, 4)
    lo = load(wo_hbm, WO, 5)
    for c in lx + [lk, lv, lq, lo]:
        c.start()

    barrier = pltpu.get_barrier_semaphore()

    @pl.loop(1, ne)
    def _(d):
        pl.semaphore_signal(barrier, inc=1, device_id=(lax.rem(e + d, ne), g), device_id_type=MESH)

    @pl.loop(1, ng)
    def _(d):
        pl.semaphore_signal(barrier, inc=1, device_id=(e, lax.rem(g + d, ng)), device_id_type=MESH)

    @pl.when(jnp.logical_not(has_far))
    def _():
        X[0:2] = jnp.zeros((2, 128, 1024), BF16)
        GF[0:2] = jnp.zeros((2, 128, 128), BF16)
        LR[0] = jnp.full((3, 8, 256), BIG, F32)
        CR[0] = jnp.zeros((2, 8, 256), F32)

    for c in lx:
        c.wait()
    pl.semaphore_wait(barrier, ne - 1 + ng - 1)

    def to(src, dst, s, r, dev):
        return pltpu.make_async_remote_copy(
            src_ref=src, dst_ref=dst, send_sem=s, recv_sem=r, device_id=dev, device_id_type=MESH
        )

    x_far = [to(X.at[2], X.at[1], xs.at[0], xr.at[0], (e, far)), to(X.at[3], X.at[0], xs.at[1], xr.at[1], (e, far))]
    x_near = [to(X.at[3], X.at[4], xs.at[2], xr.at[2], (e, near)), to(X.at[2], X.at[5], xs.at[3], xr.at[3], (e, near))]

    @pl.when(has_far)
    def _():
        x_far[0].start()

    for c in x_near:
        c.start()

    def slot_of(block):
        return jnp.where(core == 0, block - (2 * g - 2), 2 * g + 3 - block)

    seen = []
    for q in range(2):
        ids = [jnp.where(core == 0, slot_of(kb_ref[q, n]), slot_of(kb_ref[1 - q, n])) for n in range(3)]
        seen.append([(ids[0] == s) | (ids[1] == s) | (ids[2] == s) for s in range(6)])

    low = lax.broadcasted_iota(jnp.int32, (1, 128), 1) < 64

    def stacked(block):
        zero = jnp.zeros_like(block)
        return jnp.concatenate([jnp.where(low, block, zero), jnp.where(low, zero, block)], axis=0)

    def rows_of(ref, slot, count):
        return ref[slot : slot + count].reshape(count * 128, 1024)

    def project_kv(W, D, DT, slot, count, group=1):
        def tile(j):
            r = nn(rows_of(X, slot, count), W[:, span(j, 256)]).astype(BF16)
            for h in range(2):
                part = r[:, h * 128 : (h + 1) * 128]
                D[2 * j + h, slot * 128 : (slot + count) * 128, :] = part
                DT[2 * j + h, :, slot * 128 : (slot + count) * 128] = part.T

        unrolled(4, group, tile)

    def project_q(slot, count, group=1):
        def tile(j):
            r = nn(rows_of(X, slot, count), WQ[:, span(j, 256)]).astype(BF16)
            r = (r.astype(F32) * 0.125).astype(BF16)
            for h in range(2):
                for i in range(count):
                    QQ[2 * j + h, slot + i] = stacked(r[i * 128 : (i + 1) * 128, h * 128 : (h + 1) * 128])

        unrolled(4, group, tile)

    def attend(qi, first, last, step, final, group=1):
        n = last - first + 1
        off = (first - qi) * 128

        def head_pair(hp):
            row = pl.ds(hp, 1)
            s = nt(K[hp, first * 128 : (last + 1) * 128, :], QQ[hp, 2 + qi])
            if step:
                m_old = MS[qi, step - 1, row, :]
                m = m_old
            else:
                m = jnp.full((1, 256), NEG, F32)
            parts = [s[i * 128 : (i + 1) * 128] for i in range(n)]
            for i, part in enumerate(parts):
                m = jnp.maximum(m, jnp.where(seen[qi][first + i], jnp.max(part, axis=0, keepdims=True), NEG))
            total = jnp.zeros((1, 256), F32)
            exps = []
            for i, part in enumerate(parts):
                x = jnp.exp(part - jnp.where(seen[qi][first + i], m, BIG))
                total = total + jnp.sum(x, axis=0, keepdims=True)
                exps.append(x.astype(BF16))
            eb = jnp.concatenate(exps, axis=0) if n > 1 else exps[0]
            E[qi, hp, off : off + n * 128, :] = eb
            acc = diagonal(nn(VT[hp, :, first * 128 : (last + 1) * 128], eb))
            if step:
                alpha = jnp.exp(m_old - m)
                total = total + L[qi, row, :] * alpha
                acc = acc + ACC[qi, hp] * heads_of(alpha)
            MS[qi, step, row, :] = m
            if final:
                LSE[qi, row, :] = m + jnp.log(total)
                mix = (acc * heads_of(1.0 / total)).T
                lanes = span(hp, 128)
                MIXF[qi, :, lanes] = mix
                MIXB[qi, :, lanes] = mix.astype(BF16)
            else:
                L[qi, row, :] = total
                ACC[qi, hp] = acc

        unrolled(8, group, head_pair)

    def decode(qi):
        f = nt(MIXB[qi], MW[...])
        FC[qi] = (FX[qi] + (f[:, :128] + f[:, 128:])).astype(BF16)

    def place(t):
        half = t // 8
        return jnp.where(core == 0, half, 1 - half), pl.multiple_of(lax.rem(t, 8) * 16, 16)

    def a1(d):
        t = lax.rem(e + d, ne)
        b, r = place(t)
        return to(FC.at[b, pl.ds(r, 16)], RV.at[e], a1s.at[d], a1r.at[d], (t, g))

    lk.wait()
    lv.wait()
    project_kv(WK, K, KT, 2, 2)
    project_kv(WV, V, VT, 2, 2)
    lq.wait()
    project_q(2, 2)
    for c in x_near:
        c.wait_recv()
    project_kv(WK, K, KT, 4, 2)
    project_kv(WV, V, VT, 4, 2)
    attend(0, 2, 4, 0, False)

    @pl.when(has_far)
    def _():
        x_far[0].wait_send()
        x_far[1].start()

    attend(1, 2, 5, 0, False)
    project_q(4, 2)
    MP[...] = jnp.concatenate([decoder_ref[...], jnp.zeros((28, 1024), BF16)], axis=0)
    TT[...] = jnp.concatenate([targets_ref[...], jnp.zeros((28, 256), F32)], axis=0).T
    lo.wait()

    @pl.loop(0, 4)
    def _(j):
        r = nt(MP[...], WO[span(j, 256), :])
        hi = r.astype(BF16)
        MW[0:128, span(j, 256)] = hi
        MW[128:256, span(j, 256)] = (r - hi.astype(F32)).astype(BF16)

    for qi in range(2):
        FX[qi] = nt(X[2 + qi], MP[...])

    @pl.when(has_far)
    def _():
        x_far[0].wait_recv()

    project_kv(WK, K, KT, 1, 1, 4)
    project_kv(WV, V, VT, 1, 1, 4)
    attend(1, 1, 1, 1, True, UNROLL)
    attend(0, 1, 1, 1, False, UNROLL)
    decode(1)

    @pl.when(has_far)
    def _():
        x_far[1].wait_recv()

    project_kv(WK, K, KT, 0, 1, 4)
    project_kv(WV, V, VT, 0, 1, 4)
    attend(0, 0, 0, 2, True, UNROLL)
    decode(0)

    @pl.loop(1, ne)
    def _(d):
        a1(d).start()

    b_own, r_own = place(e)
    RV[e] = FC[b_own, pl.ds(r_own, 16), :]

    def shown(qi, s):
        return jnp.where(seen[qi][s], LSE[qi], BIG)

    LO[0, 0], LO[0, 1], LO[0, 2] = shown(0, 1), shown(0, 0), shown(1, 1)
    LO[1, 0], LO[1, 1], LO[1, 2] = shown(1, 5), shown(1, 4), shown(0, 4)
    l_far = to(LO.at[0], LR.at[0], ls.at[0], lr.at[0], (e, far))
    l_near = to(LO.at[1], LR.at[1], ls.at[1], lr.at[1], (e, near))

    @pl.when(has_far)
    def _():
        l_far.start()

    l_near.start()

    @pl.loop(0, 8)
    def _(hp):
        row = pl.ds(hp, 1)
        for qi in range(2):
            lse = LSE[qi, row, :]
            spans = ((2, 4), (1, 1), (0, 0)) if qi == 0 else ((2, 5), (1, 1))
            for step, (first, last) in enumerate(spans):
                scale = jnp.exp(MS[qi, step, row, :] - lse)
                a, b = (first - qi) * 128, (last + 1 - qi) * 128
                E[qi, hp, a:b, :] = (E[qi, hp, a:b, :].astype(F32) * scale).astype(BF16)

    project_q(0, 2)

    sides = ((1, 0, 256), (4, 5, 384))

    def foreign(side):
        q1, q2, k2 = sides[side]

        @pl.loop(0, 8)
        def _(hp):
            row = pl.ds(hp, 1)
            s1 = nt(K[hp, 256:512, :], QQ[hp, q1])
            PF[side, hp, 0:128] = jnp.exp(s1[:128] - LR[side, 0, row, :]).astype(BF16)
            PF[side, hp, 128:256] = jnp.exp(s1[128:] - LR[side, 1, row, :]).astype(BF16)
            s2 = nt(K[hp, k2 : k2 + 128, :], QQ[hp, q2])
            PF[side, hp, 256:384] = jnp.exp(s2 - LR[side, 2, row, :]).astype(BF16)

    l_near.wait_recv()
    foreign(1)

    @pl.loop(1, ne)
    def _(d):
        a1(d).wait_recv()

    Y[...] = RV[...].astype(F32)
    truth = TT[pl.ds(pl.multiple_of(e * 16, 16), 16), :]
    line = lax.broadcasted_iota(jnp.int32, (16, 128), 0)
    weight = jnp.zeros((16, 128), F32)
    for i in range(16):
        weight = jnp.where(line == i, area_ref[e * 16 + i], weight)
    weight = jnp.where(lax.broadcasted_iota(jnp.int32, (16, 128), 1) < variables, weight, 0.0)

    def score(i, total):
        y = Y[i]
        d = y - truth
        v = d * d + SMOOTH * SMOOTH
        r = lax.rsqrt(v)
        pd = y[None] - Y[...]
        pv = pd * pd + SMOOTH * SMOOTH
        pr = lax.rsqrt(pv)
        grad = weight * (d * r - jnp.sum(pd * pr, axis=0) / (ne - 1))
        G[i] = grad.astype(BF16)
        return total + (v * r - jnp.sum(pv * pr, axis=0) / (2.0 * (ne - 1)))

    total = lax.fori_loop(0, ne, score, jnp.zeros((16, 128), F32))
    partial = jnp.sum(jnp.sum(total * weight, axis=0, keepdims=True), axis=1, keepdims=True)
    p_hi = partial.astype(BF16).astype(F32)
    p_mid = (partial - p_hi).astype(BF16).astype(F32)
    p_lo = partial - p_hi - p_mid
    lane = lax.broadcasted_iota(jnp.int32, (16, 128), 1)
    first_row = lax.broadcasted_iota(jnp.int32, (16, 128), 0) == 0
    rider = jnp.where(lane == 104, p_hi, jnp.where(lane == 105, p_mid, jnp.where(lane == 106, p_lo, 0.0)))
    rider = jnp.where(first_row, rider, 0.0)

    def ride(i, carry):
        G[i] = (G[i].astype(F32) + rider).astype(BF16)
        return carry

    lax.fori_loop(0, ne, ride, 0)

    def a2(d):
        t = lax.rem(e + d, ne)
        b, r = place(e)
        return to(G.at[t], GF.at[2 + b, pl.ds(r, 16)], a2s.at[d], a2r.at[d], (t, g))

    @pl.loop(1, ne)
    def _(d):
        a2(d).start()

    GF[2 + b_own, pl.ds(r_own, 16), :] = G[e]

    @pl.when(has_far)
    def _():
        l_far.wait_recv()

    foreign(0)

    def a2_in(d):
        b, r = place(lax.rem(e - d + ne, ne))
        return to(G.at[0], GF.at[2 + b, pl.ds(r, 16)], a2s.at[d], a2r.at[d], (e, g))

    @pl.loop(1, ne)
    def _(d):
        a2_in(d).wait_recv()

    g_far = [to(GF.at[2], GF.at[1], gs.at[0], gr.at[0], (e, far)), to(GF.at[3], GF.at[0], gs.at[1], gr.at[1], (e, far))]
    g_near = [to(GF.at[3], GF.at[4], gs.at[2], gr.at[2], (e, near)), to(GF.at[2], GF.at[5], gs.at[3], gr.at[3], (e, near))]

    @pl.when(has_far)
    def _():
        for c in g_far:
            c.start()

    for c in g_near:
        c.start()

    mine = GF[2:4].reshape(256, 128).astype(F32)
    lane = lax.broadcasted_iota(jnp.int32, (256, 128), 1)
    mine = jnp.where((lane >= 104) & (lane < 107), mine, 0.0)
    band = jnp.sum(jnp.sum(mine, axis=0, keepdims=True), axis=1, keepdims=True)
    LS[g] = jnp.broadcast_to(band, (8, 128))

    def tell(d):
        return to(LS.at[g], LS.at[g], ts.at[d], tr.at[d], (e, lax.rem(g + d, ng)))

    def told(d):
        s = lax.rem(g - d + ng, ng)
        return to(LS.at[s], LS.at[s], ts.at[d], tr.at[d], (e, g))

    @pl.loop(1, ng)
    def _(d):
        tell(d).start()

    pair_of = lax.broadcasted_iota(jnp.int32, (16, 1024), 0)
    pair_of = 2 * lax.rem(pair_of, 8) + pair_of // 8
    indicator = jnp.where(lax.broadcasted_iota(jnp.int32, (16, 1024), 1) // 64 == pair_of, 1.0, 0.0).astype(BF16)

    def d_mix(slot, count, own):
        rows = GF[slot : slot + count].reshape(count * 128, 128)
        twice = jnp.concatenate([rows, rows], axis=1)
        c = jnp.zeros((16, 256), F32)
        for j in range(4):
            r = nn(twice, MW[:, span(j, 256)]).astype(BF16)
            for h in range(2):
                for i in range(count):
                    DD[2 * j + h, slot + i] = stacked(r[i * 128 : (i + 1) * 128, h * 128 : (h + 1) * 128])
            if own:
                prod = r.astype(F32) * MIXF[:, :, span(j, 256)].reshape(256, 256)
                hi = prod.astype(BF16)
                lower = (prod - hi.astype(F32)).astype(BF16)
                c = c + nt(indicator[:, span(j, 256)], hi) + nt(indicator[:, span(j, 256)], lower)
        if own:
            for i in range(2):
                C[i] = jnp.concatenate([c[0:8, span(i, 128)], c[8:16, span(i, 128)]], axis=1)

    d_mix(2, 2, True)
    c_far = to(C, CR.at[0], cs.at[0], cr.at[0], (e, far))
    c_near = to(C, CR.at[1], cs.at[1], cr.at[1], (e, near))

    @pl.when(has_far)
    def _():
        c_far.start()

    c_near.start()

    def own_back(hp):
        row = pl.ds(hp, 1)
        dk = jnp.zeros((256, 128), F32)
        dv = jnp.zeros((256, 128), F32)
        for qi in range(2):
            window = slice(qi * 128, qi * 128 + 640)
            dp = nt(V[hp, window, :], DD[hp, 2 + qi])
            p = E[qi, hp]
            ds = (p.astype(F32) * (dp - C[qi, row, :])).astype(BF16)
            dq = diagonal(nn(KT[hp, :, window], ds)).T * 0.125
            DQ[qi, :, span(hp, 128)] = dq.astype(BF16)
            own = slice((2 - qi) * 128, (4 - qi) * 128)
            dk = dk + nn(ds[own], QQ[hp, 2 + qi])
            dv = dv + nn(p[own], DD[hp, 2 + qi])
        DK[hp] = dk
        DV[hp] = dv

    unrolled(8, UNROLL_OWN, own_back)

    def foreign_back(side, final):
        q1, q2, k2 = sides[side]
        c1, c2 = (0, 1) if side == 0 else (1, 0)

        def head_pair(hp):
            row = pl.ds(hp, 1)
            p1 = PF[side, hp, 0:256]
            ds1 = (p1.astype(F32) * (nt(V[hp, 256:512, :], DD[hp, q1]) - CR[side, c1, row, :])).astype(BF16)
            dk = DK[hp] + nn(ds1, QQ[hp, q1])
            dv = DV[hp] + nn(p1, DD[hp, q1])
            p2 = PF[side, hp, 256:384]
            ds2 = (p2.astype(F32) * (nt(V[hp, k2 : k2 + 128, :], DD[hp, q2]) - CR[side, c2, row, :])).astype(BF16)
            dk2 = nn(ds2, QQ[hp, q2])
            dv2 = nn(p2, DD[hp, q2])
            if side == 0:
                dk = jnp.concatenate([dk[:128] + dk2, dk[128:]], axis=0)
                dv = jnp.concatenate([dv[:128] + dv2, dv[128:]], axis=0)
            else:
                dk = jnp.concatenate([dk[:128], dk[128:] + dk2], axis=0)
                dv = jnp.concatenate([dv[:128], dv[128:] + dv2], axis=0)
            if final:
                lanes = span(hp, 128)
                DKB[:, lanes] = dk.astype(BF16)
                DVB[:, lanes] = dv.astype(BF16)
            else:
                DK[hp] = dk
                DV[hp] = dv

        unrolled(8, UNROLL_BACK, head_pair)

    for c in g_near:
        c.wait_recv()
    d_mix(4, 2, False)
    c_near.wait_recv()
    foreign_back(1, False)

    for j in range(4):
        lanes = span(j, 256)
        own_rows = GF[2:4].reshape(256, 128)
        DO[:, lanes] = nn(own_rows, MP[:, lanes]) + nt(DQ[...].reshape(256, 1024), WQ[lanes, :])

    @pl.when(has_far)
    def _():
        for c in g_far:
            c.wait_recv()

    d_mix(0, 2, False)

    @pl.when(has_far)
    def _():
        c_far.wait_recv()

    foreign_back(0, True)

    for j in range(4):
        lanes = span(j, 256)
        r = (DO[:, lanes] + nt(DKB[...], WK[lanes, :]) + nt(DVB[...], WV[lanes, :])).astype(BF16)
        out_ref[pl.ds(pl.multiple_of(core * 128, 128), 128), lanes] = r[:128]
        out_ref[pl.ds(pl.multiple_of((1 - core) * 128, 128), 128), lanes] = r[128:]

    @pl.loop(1, ng)
    def _(d):
        told(d).wait_recv()

    loss_ref[...] = jnp.sum(LS[...], axis=0)[0:1, 0:1] * (1.0 / (256 * ng * variables))

    @pl.when(has_far)
    def _():
        for c in [x_far[1]] + g_far + [l_far, c_far]:
            c.wait_send()

    for c in x_near + g_near + [l_near, c_near]:
        c.wait_send()

    @pl.loop(1, ne)
    def _(d):
        a1(d).wait_send()
        a2(d).wait_send()

    @pl.loop(1, ng)
    def _(d):
        tell(d).wait_send()


def shards(x, wq, wk, wv, wo, decoder, targets, area_weight, key_blocks):
    ne, ng = lax.axis_size("ens"), lax.axis_size("grid")
    points, channels = x.shape[1:]
    variables = decoder.shape[0]
    vm = pltpu.VMEM
    dma = pltpu.SemaphoreType.DMA
    scratch = [vm((1024, 1024), BF16)] * 4 + [
        vm((128, 1024), BF16),
        vm((256, 1024), BF16),
        vm((256, 128), F32),
        vm((6, 128, 1024), BF16),
        vm((8, 768, 128), BF16),
        vm((8, 768, 128), BF16),
        vm((8, 128, 768), BF16),
        vm((8, 128, 768), BF16),
        vm((8, 6, 256, 128), BF16),
        vm((8, 6, 256, 128), BF16),
        vm((2, 8, 640, 256), BF16),
        vm((2, 8, 128, 128), F32),
        vm((2, 3, 8, 256), F32),
        vm((2, 8, 256), F32),
        vm((2, 8, 256), F32),
        vm((2, 3, 8, 256), F32),
        vm((2, 3, 8, 256), F32),
        vm((2, 128, 1024), F32),
        vm((2, 128, 1024), BF16),
        vm((2, 128, 128), F32),
        vm((2, 128, 128), BF16),
        vm((16, 16, 128), BF16),
        vm((16, 16, 128), F32),
        vm((16, 16, 128), BF16),
        vm((6, 128, 128), BF16),
        vm((2, 8, 384, 256), BF16),
        vm((256, 1024), F32),
        vm((2, 128, 1024), BF16),
        vm((8, 256, 128), F32),
        vm((8, 256, 128), F32),
        vm((256, 1024), BF16),
        vm((256, 1024), BF16),
        vm((2, 8, 256), F32),
        vm((2, 2, 8, 256), F32),
        vm((16, 8, 128), F32),
        dma((7,)),
        dma((4,)),
        dma((4,)),
        dma((16,)),
        dma((16,)),
        dma((16,)),
        dma((16,)),
        dma((4,)),
        dma((4,)),
        dma((2,)),
        dma((2,)),
        dma((2,)),
        dma((2,)),
        dma((16,)),
        dma((16,)),
    ]
    anywhere = pl.BlockSpec(memory_space=pl.ANY)
    in_vmem = pl.BlockSpec(memory_space=pltpu.VMEM)
    grad, loss = pl.pallas_call(
        functools.partial(kernel, ne, ng, variables),
        out_shape=(
            jax.ShapeDtypeStruct((points, channels), BF16),
            jax.ShapeDtypeStruct((1, 1), F32),
        ),
        in_specs=[pl.BlockSpec(memory_space=pltpu.SMEM)] * 2 + [anywhere] * 5 + [in_vmem] * 2,
        out_specs=(in_vmem, in_vmem),
        scratch_shapes=scratch,
        compiler_params=pltpu.CompilerParams(
            collective_id=0, has_side_effects=True, vmem_limit_bytes=58 * 1024 * 1024
        ),
        name="whole",
    )(key_blocks, area_weight, x[0], wq, wk, wv, wo, decoder, targets)
    return grad[None], loss[0, 0]


def solution(mesh):
    return jax.shard_map(
        shards,
        mesh=mesh,
        in_specs=(
            P("ens", "grid", None),
            P(),
            P(),
            P(),
            P(),
            P(),
            P(None, "grid"),
            P("grid"),
            P("grid", None),
        ),
        out_specs=(P("ens", "grid", None), P()),
        check_vma=False,
    )
```

```python
import functools

import jax
import jax.numpy as jnp
from jax import lax
from jax.experimental import pallas as pl
from jax.experimental.pallas import tpu as pltpu
from jax.sharding import PartitionSpec as P

MESH = pl.DeviceIdType.MESH
SMOOTH = 0.25
BIG = 1e30
NEG = -1e30
F32 = jnp.float32
BF16 = jnp.bfloat16
UNROLL = 8
UNROLL_OWN = 8
UNROLL_BACK = 8


def nt(a, b):
    return lax.dot_general(a, b, (((1,), (1,)), ((), ())), preferred_element_type=F32)


def nn(a, b):
    return lax.dot_general(a, b, (((1,), (0,)), ((), ())), preferred_element_type=F32)


def heads_of(row):
    return jnp.concatenate(
        [
            jnp.broadcast_to(row[:, :128], (64, 128)),
            jnp.broadcast_to(row[:, 128:], (64, 128)),
        ],
        axis=0,
    )


def diagonal(pair):
    return jnp.concatenate([pair[:64, :128], pair[64:, 128:]], axis=0)


def unrolled(count, group, body):
    if group == count:
        for i in range(count):
            body(i)
    else:

        @pl.loop(0, count // group)
        def _(k):
            for i in range(group):
                body(k * group + i)


def span(i, width):
    if isinstance(i, int):
        return slice(i * width, (i + 1) * width)
    return pl.ds(pl.multiple_of(i * width, width), width)


def kernel(
    ne,
    ng,
    variables,
    kb_ref,
    area_ref,
    x_hbm,
    wq_hbm,
    wk_hbm,
    wv_hbm,
    wo_hbm,
    decoder_ref,
    targets_ref,
    out_ref,
    loss_ref,
    WQ,
    WK,
    WV,
    WO,
    MP,
    MW,
    TT,
    X,
    K,
    V,
    KT,
    VT,
    QQ,
    DD,
    E,
    ACC,
    MS,
    L,
    LSE,
    SO,
    SR,
    LB,
    PS,
    PR,
    MXF,
    LO,
    LR,
    LF,
    LFR,
    MIXF,
    MIXB,
    FX,
    FC,
    RV,
    Y,
    G,
    GF,
    PF,
    DO,
    DQ,
    DK,
    DV,
    DKB,
    DVB,
    C,
    CR,
    LS,
    loc,
    xs,
    xr,
    a1s,
    a1r,
    a2s,
    a2r,
    gs,
    gr,
    ls,
    lr,
    ps,
    pr,
    cs,
    cr,
    ts,
    tr,
):
    e = lax.axis_index("ens")
    g = lax.axis_index("grid")
    core = lax.rem(g, 2)
    far = g - 1 + 2 * core
    near = g + 1 - 2 * core
    has_far = (far >= 0) & (far < ng)

    def load(src, dst, i):
        return pltpu.make_async_copy(src, dst, loc.at[i])

    lx = [
        load(x_hbm.at[pl.ds(pl.multiple_of(core * 128, 128), 128)], X.at[2], 0),
        load(x_hbm.at[pl.ds(pl.multiple_of((1 - core) * 128, 128), 128)], X.at[3], 1),
    ]
    lk, lv, lq = load(wk_hbm, WK, 2), load(wv_hbm, WV, 3), load(wq_hbm, WQ, 4)
    lo = load(wo_hbm, WO, 5)
    for c in lx + [lk, lv, lq, lo]:
        c.start()

    barrier = pltpu.get_barrier_semaphore()

    @pl.loop(1, ne)
    def _(d):
        pl.semaphore_signal(barrier, inc=1, device_id=(lax.rem(e + d, ne), g), device_id_type=MESH)

    @pl.loop(1, ng)
    def _(d):
        pl.semaphore_signal(barrier, inc=1, device_id=(e, lax.rem(g + d, ng)), device_id_type=MESH)

    @pl.when(jnp.logical_not(has_far))
    def _():
        X[0:2] = jnp.zeros((2, 128, 1024), BF16)
        GF[0:2] = jnp.zeros((2, 128, 128), BF16)
        LFR[...] = jnp.full((8, 256), BIG, F32)
        SR[0] = jnp.zeros((8, 256), F32)
        SR[1] = jnp.ones((8, 256), F32)
        SR[2:4] = jnp.full((2, 8, 256), BIG, F32)
        PR[...] = jnp.zeros((128, 128), BF16)
        CR[0] = jnp.zeros((2, 8, 256), F32)

    for c in lx:
        c.wait()
    pl.semaphore_wait(barrier, ne - 1 + ng - 1)

    def to(src, dst, s, r, dev):
        return pltpu.make_async_remote_copy(
            src_ref=src, dst_ref=dst, send_sem=s, recv_sem=r, device_id=dev, device_id_type=MESH
        )

    x_far = [to(X.at[2], X.at[1], xs.at[0], xr.at[0], (e, far)), to(X.at[3], X.at[0], xs.at[1], xr.at[1], (e, far))]
    x_near = [to(X.at[3], X.at[4], xs.at[2], xr.at[2], (e, near)), to(X.at[2], X.at[5], xs.at[3], xr.at[3], (e, near))]

    @pl.when(has_far)
    def _():
        x_far[0].start()

    for c in x_near:
        c.start()

    def slot_of(block):
        return jnp.where(core == 0, block - (2 * g - 2), 2 * g + 3 - block)

    seen, picked = [], []
    for q in range(2):
        ids = [jnp.where(core == 0, slot_of(kb_ref[q, n]), slot_of(kb_ref[1 - q, n])) for n in range(3)]
        picked.append([jnp.clip(i, q, q + 4) for i in ids])
        seen.append([(ids[0] == s) | (ids[1] == s) | (ids[2] == s) for s in range(6)])

    low = lax.broadcasted_iota(jnp.int32, (1, 128), 1) < 64

    def stacked(block):
        zero = jnp.zeros_like(block)
        return jnp.concatenate([jnp.where(low, block, zero), jnp.where(low, zero, block)], axis=0)

    def rows_of(ref, slot, count):
        return ref[slot : slot + count].reshape(count * 128, 1024)

    def project_kv(slot, count, group=1):
        def tile(j):
            rows = slice(slot * 128, (slot + count) * 128)
            k = nn(rows_of(X, slot, count), WK[:, span(j, 256)]).astype(BF16)
            v = nn(rows_of(X, slot, count), WV[:, span(j, 256)]).astype(BF16)
            for h in range(2):
                part = k[:, span(h, 128)]
                K[2 * j + h, rows, :] = part
                for i in range(count):
                    KT[2 * j + h, slot + i] = part[span(i, 128)].T
                part = v[:, span(h, 128)]
                V[2 * j + h, slot : slot + count] = part.reshape(count, 128, 128)
                VT[2 * j + h, :, rows] = part.T

        unrolled(4, group, tile)

    def project_q(slot, count, group=1):
        def tile(j):
            r = nn(rows_of(X, slot, count), WQ[:, span(j, 256)]).astype(BF16)
            r = (r.astype(F32) * 0.125).astype(BF16)
            for h in range(2):
                for i in range(count):
                    QQ[2 * j + h, slot + i] = stacked(r[i * 128 : (i + 1) * 128, h * 128 : (h + 1) * 128])

        unrolled(4, group, tile)

    def attend(qi, first, last, step, final, group=1):
        n = last - first + 1
        off = first - qi

        def head_pair(hp):
            row = pl.ds(hp, 1)
            s = nt(K[hp, first * 128 : (last + 1) * 128, :], QQ[hp, 2 + qi])
            if step:
                m_old = MS[qi, step - 1, row, :]
                m = m_old
            else:
                m = jnp.full((1, 256), NEG, F32)
            parts = [s[i * 128 : (i + 1) * 128] for i in range(n)]
            for i, part in enumerate(parts):
                m = jnp.maximum(m, jnp.where(seen[qi][first + i], jnp.max(part, axis=0, keepdims=True), NEG))
            total = jnp.zeros((1, 256), F32)
            exps = []
            for i, part in enumerate(parts):
                x = jnp.exp(part - jnp.where(seen[qi][first + i], m, BIG))
                total = total + jnp.sum(x, axis=0, keepdims=True)
                exps.append(x.astype(BF16))
            eb = jnp.concatenate(exps, axis=0) if n > 1 else exps[0]
            E[qi, hp, off : off + n] = eb.reshape(n, 128, 256)
            acc = diagonal(nn(VT[hp, :, first * 128 : (last + 1) * 128], eb))
            if step:
                alpha = jnp.exp(m_old - m)
                total = total + L[qi, row, :] * alpha
                acc = acc + ACC[qi, hp] * heads_of(alpha)
            MS[qi, step, row, :] = m
            if final:
                LSE[qi, row, :] = m + jnp.log(total)
                mix = (acc * heads_of(1.0 / total)).T
                lanes = span(hp, 128)
                MIXF[qi, :, lanes] = mix
                MIXB[qi, :, lanes] = mix.astype(BF16)
            else:
                L[qi, row, :] = total
                ACC[qi, hp] = acc

        unrolled(8, group, head_pair)

    def decode(qi):
        f = nt(MIXB[qi], MW[...])
        FC[qi] = (FX[qi] + (f[:, :128] + f[:, 128:])).astype(BF16)

    def place(t):
        half = t // 8
        return jnp.where(core == 0, half, 1 - half), pl.multiple_of(lax.rem(t, 8) * 16, 16)

    def a1(d):
        t = lax.rem(e + d, ne)
        b, r = place(t)
        return to(FC.at[b, pl.ds(r, 16)], RV.at[e], a1s.at[d], a1r.at[d], (t, g))

    lk.wait()
    lv.wait()
    project_kv(2, 2)
    lq.wait()
    project_q(2, 2)
    for c in x_near:
        c.wait_recv()
    project_kv(4, 2)
    attend(0, 2, 4, 0, False)
    SO[0] = MS[0, 0]
    SO[1] = L[0]
    SO[2] = jnp.full((8, 256), jnp.where(seen[0][1], 0.0, BIG), F32)
    SO[3] = jnp.full((8, 256), jnp.where(seen[0][0], 0.0, BIG), F32)
    s_far = to(SO, SR, ps.at[0], pr.at[0], (e, far))

    @pl.when(has_far)
    def _():
        s_far.start()

    attend(1, 2, 5, 0, False)
    project_q(4, 2)
    MP[...] = jnp.concatenate([decoder_ref[...], jnp.zeros((28, 1024), BF16)], axis=0)
    TT[...] = jnp.concatenate([targets_ref[...], jnp.zeros((28, 256), F32)], axis=0).T
    lo.wait()

    @pl.loop(0, 4)
    def _(j):
        r = nt(MP[...], WO[span(j, 256), :])
        hi = r.astype(BF16)
        MW[0:128, span(j, 256)] = hi
        MW[128:256, span(j, 256)] = (r - hi.astype(F32)).astype(BF16)

    for qi in range(2):
        FX[qi] = nt(X[2 + qi], MP[...])

    @pl.when(has_far)
    def _():
        x_far[0].wait_send()
        x_far[1].start()
        x_far[0].wait_recv()
        s_far.wait_recv()

    def far_query(hp):
        row = pl.ds(hp, 1)
        s = nt(K[hp, 256:512, :], QQ[hp, 1])
        m_old, bias_a, bias_b = SR[0, row, :], SR[2, row, :], SR[3, row, :]
        m = jnp.maximum(m_old, jnp.max(s[:128], axis=0, keepdims=True) - bias_a)
        m = jnp.maximum(m, jnp.max(s[128:], axis=0, keepdims=True) - bias_b)
        xa, xb = jnp.exp(s[:128] - (m + bias_a)), jnp.exp(s[128:] - (m + bias_b))
        total = SR[1, row, :] * jnp.exp(m_old - m)
        total = total + jnp.sum(xa, axis=0, keepdims=True) + jnp.sum(xb, axis=0, keepdims=True)
        LB[0, row, :] = m + jnp.log(total)
        p = (jnp.concatenate([xa, xb], axis=0) * (1.0 / total)).astype(BF16)
        PF[0, hp, 0:256] = p
        MXF[:, span(hp, 128)] = diagonal(nn(VT[hp, :, 256:512], p)).T.astype(BF16)

    project_q(1, 1, 4)
    unrolled(8, UNROLL, far_query)
    f = nt(MXF[...], MW[...])
    PS[...] = (f[:, :128] + f[:, 128:]).astype(BF16)
    p_far = [to(PS, PR, ps.at[1], pr.at[1], (e, far)), to(LB.at[0], LB.at[1], ps.at[2], pr.at[2], (e, far))]

    @pl.when(has_far)
    def _():
        for c in p_far:
            c.start()

    @pl.when(jnp.logical_not(has_far))
    def _():
        LB[1] = MS[0, 0] + jnp.log(L[0])

    project_kv(1, 1, 4)
    attend(1, 1, 1, 1, True, UNROLL)
    decode(1)

    def a1_half(near_block):
        half = jnp.where(near_block, 1 - core, core)

        @pl.loop(0, 8)
        def _(i):
            t = half * 8 + i

            @pl.when(t != e)
            def _():
                a1(lax.rem(t - e + ne, ne)).start()

    a1_half(True)

    def normalise(qi, hp, spans):
        row = pl.ds(hp, 1)
        lse = LSE[qi, row, :]
        for step, (first, last) in enumerate(spans):
            scale = jnp.exp(MS[qi, step, row, :] - lse)
            a, b = first - qi, last + 1 - qi
            E[qi, hp, a:b] = (E[qi, hp, a:b].astype(F32) * scale).astype(BF16)

    @pl.loop(0, 8)
    def _(hp):
        normalise(1, hp, ((2, 5), (1, 1)))

    @pl.when(has_far)
    def _():
        for c in p_far:
            c.wait_recv()

    LSE[0] = LB[1]

    def far_block(hp):
        row = pl.ds(hp, 1)
        mix = (ACC[0, hp] * heads_of(jnp.exp(MS[0, 0, row, :] - LSE[0, row, :]))).T
        MIXF[0, :, span(hp, 128)] = mix
        MIXB[0, :, span(hp, 128)] = mix.astype(BF16)

    unrolled(8, 8, far_block)
    f = nt(MIXB[0], MW[...])
    FC[0] = (FX[0] + (f[:, :128] + f[:, 128:]) + PR[...].astype(F32)).astype(BF16)
    a1_half(False)

    b_own, r_own = place(e)
    RV[e] = FC[b_own, pl.ds(r_own, 16), :]

    def shown(qi, s):
        return jnp.where(seen[qi][s], LSE[qi], BIG)

    LF[...] = shown(1, 1)
    LO[0], LO[1], LO[2] = shown(1, 5), shown(1, 4), shown(0, 4)
    l_far = to(LF, LFR, ls.at[0], lr.at[0], (e, far))
    l_near = to(LO, LR, ls.at[1], lr.at[1], (e, near))

    @pl.when(has_far)
    def _():
        l_far.start()

    l_near.start()

    @pl.loop(0, 8)
    def _(hp):
        normalise(0, hp, ((2, 4),))

    l_near.wait_recv()

    @pl.loop(0, 8)
    def _(hp):
        row = pl.ds(hp, 1)
        s1 = nt(K[hp, 256:512, :], QQ[hp, 4])
        PF[1, hp, 0:128] = jnp.exp(s1[:128] - LR[0, row, :]).astype(BF16)
        PF[1, hp, 128:256] = jnp.exp(s1[128:] - LR[1, row, :]).astype(BF16)
        s2 = nt(K[hp, 384:512, :], QQ[hp, 5])
        PF[1, hp, 256:384] = jnp.exp(s2 - LR[2, row, :]).astype(BF16)

    def second_far():
        @pl.when(has_far)
        def _():
            x_far[1].wait_recv()
            l_far.wait_recv()

        project_kv(0, 1)
        project_q(0, 1)

        @pl.loop(0, 8)
        def _(hp):
            row = pl.ds(hp, 1)
            lse = LSE[0, row, :]
            s = nt(K[hp, 0:256, :], QQ[hp, 2])
            pa = jnp.exp(s[:128] - jnp.where(seen[0][0], lse, BIG))
            pb = jnp.exp(s[128:] - jnp.where(seen[0][1], lse, BIG))
            p = jnp.concatenate([pa, pb], axis=0).astype(BF16)
            E[0, hp, 0:2] = p.reshape(2, 128, 256)
            lanes = span(hp, 128)
            MIXF[0, :, lanes] = MIXF[0, :, lanes] + diagonal(nn(VT[hp, :, 0:256], p)).T
            s2 = nt(K[hp, 256:384, :], QQ[hp, 0])
            PF[0, hp, 256:384] = jnp.exp(s2 - LFR[row, :]).astype(BF16)

    sides = ((1, 0, 2), (4, 5, 3))

    @pl.loop(1, ne)
    def _(d):
        a1(d).wait_recv()

    Y[...] = RV[...].astype(F32)
    truth = TT[pl.ds(pl.multiple_of(e * 16, 16), 16), :]
    line = lax.broadcasted_iota(jnp.int32, (16, 128), 0)
    weight = jnp.zeros((16, 128), F32)
    for i in range(16):
        weight = jnp.where(line == i, area_ref[e * 16 + i], weight)
    weight = jnp.where(lax.broadcasted_iota(jnp.int32, (16, 128), 1) < variables, weight, 0.0)

    def score(i, total):
        y = Y[i]
        d = y - truth
        v = d * d + SMOOTH * SMOOTH
        r = lax.rsqrt(v)
        pd = y[None] - Y[...]
        pv = pd * pd + SMOOTH * SMOOTH
        pr = lax.rsqrt(pv)
        grad = weight * (d * r - jnp.sum(pd * pr, axis=0) / (ne - 1))
        G[i] = grad.astype(BF16)
        return total + (v * r - jnp.sum(pv * pr, axis=0) / (2.0 * (ne - 1)))

    total = lax.fori_loop(0, ne, score, jnp.zeros((16, 128), F32))
    partial = jnp.sum(jnp.sum(total * weight, axis=0, keepdims=True), axis=1, keepdims=True)
    p_hi = partial.astype(BF16).astype(F32)
    p_mid = (partial - p_hi).astype(BF16).astype(F32)
    p_lo = partial - p_hi - p_mid
    lane = lax.broadcasted_iota(jnp.int32, (16, 128), 1)
    first_row = lax.broadcasted_iota(jnp.int32, (16, 128), 0) == 0
    rider = jnp.where(lane == 104, p_hi, jnp.where(lane == 105, p_mid, jnp.where(lane == 106, p_lo, 0.0)))
    rider = jnp.where(first_row, rider, 0.0)

    def ride(i, carry):
        G[i] = (G[i].astype(F32) + rider).astype(BF16)
        return carry

    lax.fori_loop(0, ne, ride, 0)

    def a2(d):
        t = lax.rem(e + d, ne)
        b, r = place(e)
        return to(G.at[t], GF.at[2 + b, pl.ds(r, 16)], a2s.at[d], a2r.at[d], (t, g))

    @pl.loop(1, ne)
    def _(d):
        a2(d).start()

    GF[2 + b_own, pl.ds(r_own, 16), :] = G[e]

    second_far()

    def a2_in(d):
        b, r = place(lax.rem(e - d + ne, ne))
        return to(G.at[0], GF.at[2 + b, pl.ds(r, 16)], a2s.at[d], a2r.at[d], (e, g))

    @pl.loop(1, ne)
    def _(d):
        a2_in(d).wait_recv()

    g_far = [to(GF.at[2], GF.at[1], gs.at[0], gr.at[0], (e, far)), to(GF.at[3], GF.at[0], gs.at[1], gr.at[1], (e, far))]
    g_near = [to(GF.at[3], GF.at[4], gs.at[2], gr.at[2], (e, near)), to(GF.at[2], GF.at[5], gs.at[3], gr.at[3], (e, near))]

    @pl.when(has_far)
    def _():
        for c in g_far:
            c.start()

    for c in g_near:
        c.start()

    mine = GF[2:4].reshape(256, 128).astype(F32)
    lane = lax.broadcasted_iota(jnp.int32, (256, 128), 1)
    mine = jnp.where((lane >= 104) & (lane < 107), mine, 0.0)
    band = jnp.sum(jnp.sum(mine, axis=0, keepdims=True), axis=1, keepdims=True)
    LS[g] = jnp.broadcast_to(band, (8, 128))

    def tell(d):
        return to(LS.at[g], LS.at[g], ts.at[d], tr.at[d], (e, lax.rem(g + d, ng)))

    def told(d):
        s = lax.rem(g - d + ng, ng)
        return to(LS.at[s], LS.at[s], ts.at[d], tr.at[d], (e, g))

    @pl.loop(1, ng)
    def _(d):
        tell(d).start()

    pair_of = lax.broadcasted_iota(jnp.int32, (16, 1024), 0)
    pair_of = 2 * lax.rem(pair_of, 8) + pair_of // 8
    indicator = jnp.where(lax.broadcasted_iota(jnp.int32, (16, 1024), 1) // 64 == pair_of, 1.0, 0.0).astype(BF16)

    def d_mix(slot, count, own):
        rows = GF[slot : slot + count].reshape(count * 128, 128)
        twice = jnp.concatenate([rows, rows], axis=1)
        c = jnp.zeros((16, 256), F32)
        for j in range(4):
            r = nn(twice, MW[:, span(j, 256)]).astype(BF16)
            for h in range(2):
                for i in range(count):
                    DD[2 * j + h, slot + i] = stacked(r[i * 128 : (i + 1) * 128, h * 128 : (h + 1) * 128])
            if own:
                prod = r.astype(F32) * MIXF[:, :, span(j, 256)].reshape(256, 256)
                hi = prod.astype(BF16)
                lower = (prod - hi.astype(F32)).astype(BF16)
                c = c + nt(indicator[:, span(j, 256)], hi) + nt(indicator[:, span(j, 256)], lower)
        if own:
            for i in range(2):
                C[i] = jnp.concatenate([c[0:8, span(i, 128)], c[8:16, span(i, 128)]], axis=1)

    d_mix(2, 2, True)
    c_far = to(C, CR.at[0], cs.at[0], cr.at[0], (e, far))
    c_near = to(C, CR.at[1], cs.at[1], cr.at[1], (e, near))

    @pl.when(has_far)
    def _():
        c_far.start()

    c_near.start()

    def own_back(hp):
        row = pl.ds(hp, 1)
        dks, dvs = [], []
        for qi in range(2):
            other = [jnp.where(i == 3 - qi, 1.0, 0.0) for i in picked[qi][1:]]
            dp = nt(jnp.concatenate([V[hp, i] for i in picked[qi]], axis=0), DD[hp, 2 + qi])
            p = [E[qi, hp, i - qi].astype(F32) for i in picked[qi]]
            c = C[qi, row, :]
            ds = [p[n] * (dp[n * 128 : (n + 1) * 128] - c) for n in range(3)]
            half = [x.astype(BF16) for x in ds]
            keys = jnp.concatenate([KT[hp, i] for i in picked[qi]], axis=1)
            dq = diagonal(nn(keys, jnp.concatenate(half, axis=0))).T * 0.125
            DQ[qi, :, span(hp, 128)] = dq.astype(BF16)
            pair = [half[0], (ds[1] * other[0] + ds[2] * other[1]).astype(BF16)]
            prob = [E[qi, hp, 2], (p[1] * other[0] + p[2] * other[1]).astype(BF16)]
            if qi:
                pair, prob = pair[::-1], prob[::-1]
            dks.append(nn(jnp.concatenate(pair, axis=0), QQ[hp, 2 + qi]))
            dvs.append(nn(jnp.concatenate(prob, axis=0), DD[hp, 2 + qi]))
        DK[hp] = dks[0] + dks[1]
        DV[hp] = dvs[0] + dvs[1]

    unrolled(8, UNROLL_OWN, own_back)

    def foreign_back(side, final):
        q1, q2, k2 = sides[side]
        c1, c2 = (0, 1) if side == 0 else (1, 0)

        def head_pair(hp):
            row = pl.ds(hp, 1)
            p1 = PF[side, hp, 0:256]
            ds1 = (p1.astype(F32) * (nt(V[hp, 2:4].reshape(256, 128), DD[hp, q1]) - CR[side, c1, row, :])).astype(BF16)
            dk = DK[hp] + nn(ds1, QQ[hp, q1])
            dv = DV[hp] + nn(p1, DD[hp, q1])
            p2 = PF[side, hp, 256:384]
            ds2 = (p2.astype(F32) * (nt(V[hp, k2], DD[hp, q2]) - CR[side, c2, row, :])).astype(BF16)
            dk2 = nn(ds2, QQ[hp, q2])
            dv2 = nn(p2, DD[hp, q2])
            if side == 0:
                dk = jnp.concatenate([dk[:128] + dk2, dk[128:]], axis=0)
                dv = jnp.concatenate([dv[:128] + dv2, dv[128:]], axis=0)
            else:
                dk = jnp.concatenate([dk[:128], dk[128:] + dk2], axis=0)
                dv = jnp.concatenate([dv[:128], dv[128:] + dv2], axis=0)
            if final:
                lanes = span(hp, 128)
                DKB[:, lanes] = dk.astype(BF16)
                DVB[:, lanes] = dv.astype(BF16)
            else:
                DK[hp] = dk
                DV[hp] = dv

        unrolled(8, UNROLL_BACK, head_pair)

    for c in g_near:
        c.wait_recv()
    d_mix(4, 2, False)
    c_near.wait_recv()
    foreign_back(1, False)

    for j in range(4):
        lanes = span(j, 256)
        own_rows = GF[2:4].reshape(256, 128)
        DO[:, lanes] = nn(own_rows, MP[:, lanes]) + nt(DQ[...].reshape(256, 1024), WQ[lanes, :])

    @pl.when(has_far)
    def _():
        for c in g_far:
            c.wait_recv()

    d_mix(0, 2, False)

    @pl.when(has_far)
    def _():
        c_far.wait_recv()

    foreign_back(0, True)

    for j in range(4):
        lanes = span(j, 256)
        r = (DO[:, lanes] + nt(DKB[...], WK[lanes, :]) + nt(DVB[...], WV[lanes, :])).astype(BF16)
        out_ref[pl.ds(pl.multiple_of(core * 128, 128), 128), lanes] = r[:128]
        out_ref[pl.ds(pl.multiple_of((1 - core) * 128, 128), 128), lanes] = r[128:]

    @pl.loop(1, ng)
    def _(d):
        told(d).wait_recv()

    loss_ref[...] = jnp.sum(LS[...], axis=0)[0:1, 0:1] * (1.0 / (256 * ng * variables))

    @pl.when(has_far)
    def _():
        for c in [x_far[1], s_far] + p_far + g_far + [l_far, c_far]:
            c.wait_send()

    for c in x_near + g_near + [l_near, c_near]:
        c.wait_send()

    @pl.loop(1, ne)
    def _(d):
        a1(d).wait_send()
        a2(d).wait_send()

    @pl.loop(1, ng)
    def _(d):
        tell(d).wait_send()


def shards(x, wq, wk, wv, wo, decoder, targets, area_weight, key_blocks):
    ne, ng = lax.axis_size("ens"), lax.axis_size("grid")
    points, channels = x.shape[1:]
    variables = decoder.shape[0]
    vm = pltpu.VMEM
    dma = pltpu.SemaphoreType.DMA
    scratch = [vm((1024, 1024), BF16)] * 4 + [
        vm((128, 1024), BF16),
        vm((256, 1024), BF16),
        vm((256, 128), F32),
        vm((6, 128, 1024), BF16),
        vm((8, 768, 128), BF16),
        vm((8, 6, 128, 128), BF16),
        vm((8, 6, 128, 128), BF16),
        vm((8, 128, 768), BF16),
        vm((8, 6, 256, 128), BF16),
        vm((8, 6, 256, 128), BF16),
        vm((2, 8, 5, 128, 256), BF16),
        vm((2, 8, 128, 128), F32),
        vm((2, 3, 8, 256), F32),
        vm((2, 8, 256), F32),
        vm((2, 8, 256), F32),
        vm((4, 8, 256), F32),
        vm((4, 8, 256), F32),
        vm((2, 8, 256), F32),
        vm((128, 128), BF16),
        vm((128, 128), BF16),
        vm((128, 1024), BF16),
        vm((3, 8, 256), F32),
        vm((3, 8, 256), F32),
        vm((8, 256), F32),
        vm((8, 256), F32),
        vm((2, 128, 1024), F32),
        vm((2, 128, 1024), BF16),
        vm((2, 128, 128), F32),
        vm((2, 128, 128), BF16),
        vm((16, 16, 128), BF16),
        vm((16, 16, 128), F32),
        vm((16, 16, 128), BF16),
        vm((6, 128, 128), BF16),
        vm((2, 8, 384, 256), BF16),
        vm((256, 1024), F32),
        vm((2, 128, 1024), BF16),
        vm((8, 256, 128), F32),
        vm((8, 256, 128), F32),
        vm((256, 1024), BF16),
        vm((256, 1024), BF16),
        vm((2, 8, 256), F32),
        vm((2, 2, 8, 256), F32),
        vm((16, 8, 128), F32),
        dma((7,)),
        dma((4,)),
        dma((4,)),
        dma((16,)),
        dma((16,)),
        dma((16,)),
        dma((16,)),
        dma((4,)),
        dma((4,)),
        dma((2,)),
        dma((2,)),
        dma((3,)),
        dma((3,)),
        dma((2,)),
        dma((2,)),
        dma((16,)),
        dma((16,)),
    ]
    anywhere = pl.BlockSpec(memory_space=pl.ANY)
    in_vmem = pl.BlockSpec(memory_space=pltpu.VMEM)
    grad, loss = pl.pallas_call(
        functools.partial(kernel, ne, ng, variables),
        out_shape=(
            jax.ShapeDtypeStruct((points, channels), BF16),
            jax.ShapeDtypeStruct((1, 1), F32),
        ),
        in_specs=[pl.BlockSpec(memory_space=pltpu.SMEM)] * 2 + [anywhere] * 5 + [in_vmem] * 2,
        out_specs=(in_vmem, in_vmem),
        scratch_shapes=scratch,
        compiler_params=pltpu.CompilerParams(
            collective_id=0, has_side_effects=True, vmem_limit_bytes=58 * 1024 * 1024
        ),
        name="whole",
    )(key_blocks, area_weight, x[0], wq, wk, wv, wo, decoder, targets)
    return grad[None], loss[0, 0]


def solution(mesh):
    return jax.shard_map(
        shards,
        mesh=mesh,
        in_specs=(
            P("ens", "grid", None),
            P(),
            P(),
            P(),
            P(),
            P(),
            P(None, "grid"),
            P("grid"),
            P("grid", None),
        ),
        out_specs=(P("ens", "grid", None), P()),
        check_vma=False,
    )
```

```python
import functools

import jax
import jax.numpy as jnp
from jax import lax
from jax.experimental import pallas as pl
from jax.experimental.pallas import tpu as pltpu
from jax.sharding import PartitionSpec as P

MESH = pl.DeviceIdType.MESH
SMOOTH = 0.25
BIG = 1e30
NEG = -1e30
F32 = jnp.float32
BF16 = jnp.bfloat16
UNROLL = 8
UNROLL_OWN = 8
UNROLL_BACK = 8


def nt(a, b):
    return lax.dot_general(a, b, (((1,), (1,)), ((), ())), preferred_element_type=F32)


def nn(a, b):
    return lax.dot_general(a, b, (((1,), (0,)), ((), ())), preferred_element_type=F32)


def heads_of(row):
    return jnp.concatenate(
        [
            jnp.broadcast_to(row[:, :128], (64, 128)),
            jnp.broadcast_to(row[:, 128:], (64, 128)),
        ],
        axis=0,
    )


def diagonal(pair):
    return jnp.concatenate([pair[:64, :128], pair[64:, 128:]], axis=0)


def unrolled(count, group, body):
    if group == count:
        for i in range(count):
            body(i)
    else:

        @pl.loop(0, count // group)
        def _(k):
            for i in range(group):
                body(k * group + i)


def span(i, width):
    if isinstance(i, int):
        return slice(i * width, (i + 1) * width)
    return pl.ds(pl.multiple_of(i * width, width), width)


def kernel(
    ne,
    ng,
    variables,
    kb_ref,
    area_ref,
    x_hbm,
    wq_hbm,
    wk_hbm,
    wv_hbm,
    wo_hbm,
    decoder_ref,
    targets_ref,
    out_ref,
    loss_ref,
    WQ,
    WK,
    WV,
    WO,
    MP,
    MW,
    TT,
    X,
    K,
    V,
    KT,
    VT,
    QQ,
    DD,
    E,
    ACC,
    MS,
    L,
    LSE,
    SO,
    SR,
    LB,
    PS,
    PR,
    MXF,
    LO,
    LR,
    LF,
    LFR,
    MIXF,
    MIXB,
    FX,
    FC,
    RV,
    Y,
    G,
    GF,
    PF,
    DO,
    DQ,
    DK,
    DV,
    DKB,
    DVB,
    C,
    CR,
    LS,
    loc,
    xs,
    xr,
    a1s,
    a1r,
    a2s,
    a2r,
    gs,
    gr,
    ls,
    lr,
    ps,
    pr,
    cs,
    cr,
    ts,
    tr,
):
    e = lax.axis_index("ens")
    g = lax.axis_index("grid")
    core = lax.rem(g, 2)
    far = g - 1 + 2 * core
    near = g + 1 - 2 * core
    has_far = (far >= 0) & (far < ng)

    def load(src, dst, i):
        return pltpu.make_async_copy(src, dst, loc.at[i])

    lx = [
        load(x_hbm.at[pl.ds(pl.multiple_of(core * 128, 128), 128)], X.at[2], 0),
        load(x_hbm.at[pl.ds(pl.multiple_of((1 - core) * 128, 128), 128)], X.at[3], 1),
    ]
    lk, lv, lq = load(wk_hbm, WK, 2), load(wv_hbm, WV, 3), load(wq_hbm, WQ, 4)
    lo = load(wo_hbm, WO, 5)
    for c in lx + [lk, lv, lq, lo]:
        c.start()

    barrier = pltpu.get_barrier_semaphore()

    @pl.loop(1, ne)
    def _(d):
        pl.semaphore_signal(barrier, inc=1, device_id=(lax.rem(e + d, ne), g), device_id_type=MESH)

    @pl.loop(1, ng)
    def _(d):
        pl.semaphore_signal(barrier, inc=1, device_id=(e, lax.rem(g + d, ng)), device_id_type=MESH)

    @pl.when(jnp.logical_not(has_far))
    def _():
        X[0:2] = jnp.zeros((2, 128, 1024), BF16)
        GF[0:2] = jnp.zeros((2, 128, 128), BF16)
        LFR[...] = jnp.full((8, 256), BIG, F32)
        SR[0] = jnp.zeros((8, 256), F32)
        SR[1] = jnp.ones((8, 256), F32)
        SR[2:4] = jnp.full((2, 8, 256), BIG, F32)
        PR[...] = jnp.zeros((128, 128), BF16)
        CR[0] = jnp.zeros((2, 8, 256), F32)

    for c in lx:
        c.wait()
    pl.semaphore_wait(barrier, ne - 1 + ng - 1)

    def to(src, dst, s, r, dev):
        return pltpu.make_async_remote_copy(
            src_ref=src, dst_ref=dst, send_sem=s, recv_sem=r, device_id=dev, device_id_type=MESH
        )

    x_far = [to(X.at[2], X.at[1], xs.at[0], xr.at[0], (e, far)), to(X.at[3], X.at[0], xs.at[1], xr.at[1], (e, far))]
    x_near = [to(X.at[3], X.at[4], xs.at[2], xr.at[2], (e, near)), to(X.at[2], X.at[5], xs.at[3], xr.at[3], (e, near))]

    @pl.when(has_far)
    def _():
        x_far[0].start()

    for c in x_near:
        c.start()

    def slot_of(block):
        return jnp.where(core == 0, block - (2 * g - 2), 2 * g + 3 - block)

    seen, picked = [], []
    for q in range(2):
        ids = [jnp.where(core == 0, slot_of(kb_ref[q, n]), slot_of(kb_ref[1 - q, n])) for n in range(3)]
        picked.append([jnp.clip(i, q, q + 4) for i in ids])
        seen.append([(ids[0] == s) | (ids[1] == s) | (ids[2] == s) for s in range(6)])

    low = lax.broadcasted_iota(jnp.int32, (1, 128), 1) < 64

    def stacked(block):
        zero = jnp.zeros_like(block)
        return jnp.concatenate([jnp.where(low, block, zero), jnp.where(low, zero, block)], axis=0)

    def rows_of(ref, slot, count):
        return ref[slot : slot + count].reshape(count * 128, 1024)

    def project_kv(slot, count, group=4):
        def tile(j):
            rows = slice(slot * 128, (slot + count) * 128)
            k = nn(rows_of(X, slot, count), WK[:, span(j, 256)]).astype(BF16)
            v = nn(rows_of(X, slot, count), WV[:, span(j, 256)]).astype(BF16)
            for h in range(2):
                part = k[:, span(h, 128)]
                K[2 * j + h, rows, :] = part
                for i in range(count):
                    KT[2 * j + h, slot + i] = part[span(i, 128)].T
                part = v[:, span(h, 128)]
                V[2 * j + h, slot : slot + count] = part.reshape(count, 128, 128)
                VT[2 * j + h, :, rows] = part.T

        unrolled(4, group, tile)

    def project_q(slot, count, group=4):
        def tile(j):
            r = (nn(rows_of(X, slot, count), WQ[:, span(j, 256)]) * 0.125).astype(BF16)
            for h in range(2):
                for i in range(count):
                    QQ[2 * j + h, slot + i] = stacked(r[i * 128 : (i + 1) * 128, h * 128 : (h + 1) * 128])

        unrolled(4, group, tile)

    def attend(qi, first, last, step, final, group=8):
        n = last - first + 1
        off = first - qi

        def head_pair(hp):
            row = pl.ds(hp, 1)
            s = nt(K[hp, first * 128 : (last + 1) * 128, :], QQ[hp, 2 + qi])
            if step:
                m_old = MS[qi, step - 1, row, :]
                m = m_old
            else:
                m = jnp.full((1, 256), NEG, F32)
            parts = [s[i * 128 : (i + 1) * 128] for i in range(n)]
            for i, part in enumerate(parts):
                m = jnp.maximum(m, jnp.where(seen[qi][first + i], jnp.max(part, axis=0, keepdims=True), NEG))
            total = jnp.zeros((1, 256), F32)
            exps = []
            for i, part in enumerate(parts):
                x = jnp.exp(part - jnp.where(seen[qi][first + i], m, BIG))
                total = total + jnp.sum(x, axis=0, keepdims=True)
                exps.append(x.astype(BF16))
            eb = jnp.concatenate(exps, axis=0) if n > 1 else exps[0]
            E[qi, hp, off : off + n] = eb.reshape(n, 128, 256)
            acc = diagonal(nn(VT[hp, :, first * 128 : (last + 1) * 128], eb))
            if step:
                alpha = jnp.exp(m_old - m)
                total = total + L[qi, row, :] * alpha
                acc = acc + ACC[qi, hp] * heads_of(alpha)
            MS[qi, step, row, :] = m
            if final:
                LSE[qi, row, :] = m + jnp.log(total)
                mix = (acc * heads_of(1.0 / total)).T
                lanes = span(hp, 128)
                MIXF[qi, :, lanes] = mix
                MIXB[qi, :, lanes] = mix.astype(BF16)
            else:
                L[qi, row, :] = total
                ACC[qi, hp] = acc

        unrolled(8, group, head_pair)

    def decode(qi):
        f = nt(MIXB[qi], MW[...])
        FC[qi] = (FX[qi] + (f[:, :128] + f[:, 128:])).astype(BF16)

    def place(t):
        half = t // 8
        return jnp.where(core == 0, half, 1 - half), pl.multiple_of(lax.rem(t, 8) * 16, 16)

    def a1(d):
        t = lax.rem(e + d, ne)
        b, r = place(t)
        return to(FC.at[b, pl.ds(r, 16)], RV.at[e], a1s.at[d], a1r.at[d], (t, g))

    lk.wait()
    lv.wait()
    project_kv(2, 2)
    lq.wait()
    project_q(2, 2)
    for c in x_near:
        c.wait_recv()
    project_kv(4, 2)
    attend(0, 2, 4, 0, False)
    SO[0] = MS[0, 0]
    SO[1] = L[0]
    SO[2] = jnp.full((8, 256), jnp.where(seen[0][1], 0.0, BIG), F32)
    SO[3] = jnp.full((8, 256), jnp.where(seen[0][0], 0.0, BIG), F32)
    s_far = to(SO, SR, ps.at[0], pr.at[0], (e, far))

    @pl.when(has_far)
    def _():
        s_far.start()

    attend(1, 2, 5, 0, False)
    project_q(4, 2)
    MP[...] = jnp.concatenate([decoder_ref[...], jnp.zeros((28, 1024), BF16)], axis=0)
    TT[...] = jnp.concatenate([targets_ref[...], jnp.zeros((28, 256), F32)], axis=0).T
    lo.wait()

    for j in range(4):
        r = nt(MP[...], WO[span(j, 256), :])
        hi = r.astype(BF16)
        MW[0:128, span(j, 256)] = hi
        MW[128:256, span(j, 256)] = (r - hi.astype(F32)).astype(BF16)

    for qi in range(2):
        FX[qi] = nt(X[2 + qi], MP[...])

    @pl.when(has_far)
    def _():
        x_far[0].wait_send()
        x_far[1].start()
        x_far[0].wait_recv()
        s_far.wait_recv()

    def far_query(hp):
        row = pl.ds(hp, 1)
        s = nt(K[hp, 256:512, :], QQ[hp, 1])
        m_old, bias_a, bias_b = SR[0, row, :], SR[2, row, :], SR[3, row, :]
        m = jnp.maximum(m_old, jnp.max(s[:128], axis=0, keepdims=True) - bias_a)
        m = jnp.maximum(m, jnp.max(s[128:], axis=0, keepdims=True) - bias_b)
        xa, xb = jnp.exp(s[:128] - (m + bias_a)), jnp.exp(s[128:] - (m + bias_b))
        total = SR[1, row, :] * jnp.exp(m_old - m)
        total = total + jnp.sum(xa, axis=0, keepdims=True) + jnp.sum(xb, axis=0, keepdims=True)
        LB[0, row, :] = m + jnp.log(total)
        p = (jnp.concatenate([xa, xb], axis=0) * (1.0 / total)).astype(BF16)
        PF[0, hp, 0:256] = p
        MXF[:, span(hp, 128)] = diagonal(nn(VT[hp, :, 256:512], p)).T.astype(BF16)

    project_q(1, 1, 4)
    unrolled(8, UNROLL, far_query)
    f = nt(MXF[...], MW[...])
    PS[...] = (f[:, :128] + f[:, 128:]).astype(BF16)
    p_far = [to(PS, PR, ps.at[1], pr.at[1], (e, far)), to(LB.at[0], LB.at[1], ps.at[2], pr.at[2], (e, far))]

    @pl.when(has_far)
    def _():
        for c in p_far:
            c.start()

    @pl.when(jnp.logical_not(has_far))
    def _():
        LB[1] = MS[0, 0] + jnp.log(L[0])

    project_kv(1, 1, 4)
    attend(1, 1, 1, 1, True, UNROLL)
    decode(1)

    def a1_half(near_block):
        half = jnp.where(near_block, 1 - core, core)

        @pl.loop(0, 8)
        def _(i):
            t = half * 8 + i

            @pl.when(t != e)
            def _():
                a1(lax.rem(t - e + ne, ne)).start()

    a1_half(True)

    def normalise(qi, hp, spans):
        row = pl.ds(hp, 1)
        lse = LSE[qi, row, :]
        for step, (first, last) in enumerate(spans):
            scale = jnp.exp(MS[qi, step, row, :] - lse)
            a, b = first - qi, last + 1 - qi
            E[qi, hp, a:b] = (E[qi, hp, a:b].astype(F32) * scale).astype(BF16)

    unrolled(8, 4, lambda hp: normalise(1, hp, ((2, 5), (1, 1))))

    @pl.when(has_far)
    def _():
        for c in p_far:
            c.wait_recv()

    LSE[0] = LB[1]

    def far_block(hp):
        row = pl.ds(hp, 1)
        mix = (ACC[0, hp] * heads_of(jnp.exp(MS[0, 0, row, :] - LSE[0, row, :]))).T
        MIXF[0, :, span(hp, 128)] = mix
        MIXB[0, :, span(hp, 128)] = mix.astype(BF16)

    unrolled(8, 8, far_block)
    f = nt(MIXB[0], MW[...])
    FC[0] = (FX[0] + (f[:, :128] + f[:, 128:]) + PR[...].astype(F32)).astype(BF16)
    a1_half(False)

    b_own, r_own = place(e)
    RV[e] = FC[b_own, pl.ds(r_own, 16), :]

    def shown(qi, s):
        return jnp.where(seen[qi][s], LSE[qi], BIG)

    LF[...] = shown(1, 1)
    LO[0], LO[1], LO[2] = shown(1, 5), shown(1, 4), shown(0, 4)
    l_far = to(LF, LFR, ls.at[0], lr.at[0], (e, far))
    l_near = to(LO, LR, ls.at[1], lr.at[1], (e, near))

    @pl.when(has_far)
    def _():
        l_far.start()

    l_near.start()

    unrolled(8, 4, lambda hp: normalise(0, hp, ((2, 4),)))

    l_near.wait_recv()

    def near_query(hp):
        row = pl.ds(hp, 1)
        s1 = nt(K[hp, 256:512, :], QQ[hp, 4])
        PF[1, hp, 0:128] = jnp.exp(s1[:128] - LR[0, row, :]).astype(BF16)
        PF[1, hp, 128:256] = jnp.exp(s1[128:] - LR[1, row, :]).astype(BF16)
        s2 = nt(K[hp, 384:512, :], QQ[hp, 5])
        PF[1, hp, 256:384] = jnp.exp(s2 - LR[2, row, :]).astype(BF16)

    unrolled(8, 8, near_query)

    def second_far():
        @pl.when(has_far)
        def _():
            x_far[1].wait_recv()
            l_far.wait_recv()

        project_kv(0, 1)
        project_q(0, 1)

        def head_pair(hp):
            row = pl.ds(hp, 1)
            lse = LSE[0, row, :]
            s = nt(K[hp, 0:256, :], QQ[hp, 2])
            pa = jnp.exp(s[:128] - jnp.where(seen[0][0], lse, BIG))
            pb = jnp.exp(s[128:] - jnp.where(seen[0][1], lse, BIG))
            p = jnp.concatenate([pa, pb], axis=0).astype(BF16)
            E[0, hp, 0:2] = p.reshape(2, 128, 256)
            lanes = span(hp, 128)
            MIXF[0, :, lanes] = MIXF[0, :, lanes] + diagonal(nn(VT[hp, :, 0:256], p)).T
            s2 = nt(K[hp, 256:384, :], QQ[hp, 0])
            PF[0, hp, 256:384] = jnp.exp(s2 - LFR[row, :]).astype(BF16)

        unrolled(8, 8, head_pair)

    sides = ((1, 0, 2), (4, 5, 3))

    @pl.loop(1, ne)
    def _(d):
        a1(d).wait_recv()

    Y[...] = RV[...].astype(F32)
    truth = TT[pl.ds(pl.multiple_of(e * 16, 16), 16), :]
    line = lax.broadcasted_iota(jnp.int32, (16, 128), 0)
    weight = jnp.zeros((16, 128), F32)
    for i in range(16):
        weight = jnp.where(line == i, area_ref[e * 16 + i], weight)
    weight = jnp.where(lax.broadcasted_iota(jnp.int32, (16, 128), 1) < variables, weight, 0.0)

    def score(i, total):
        y = Y[i]
        d = y - truth
        v = d * d + SMOOTH * SMOOTH
        r = lax.rsqrt(v)
        pd = y[None] - Y[...]
        pv = pd * pd + SMOOTH * SMOOTH
        pr = lax.rsqrt(pv)
        grad = weight * (d * r - jnp.sum(pd * pr, axis=0) / (ne - 1))
        G[i] = grad.astype(BF16)
        return total + (v * r - jnp.sum(pv * pr, axis=0) / (2.0 * (ne - 1)))

    total = lax.fori_loop(0, ne, score, jnp.zeros((16, 128), F32))
    partial = jnp.sum(jnp.sum(total * weight, axis=0, keepdims=True), axis=1, keepdims=True)
    p_hi = partial.astype(BF16).astype(F32)
    p_mid = (partial - p_hi).astype(BF16).astype(F32)
    p_lo = partial - p_hi - p_mid
    lane = lax.broadcasted_iota(jnp.int32, (16, 128), 1)
    first_row = lax.broadcasted_iota(jnp.int32, (16, 128), 0) == 0
    rider = jnp.where(lane == 104, p_hi, jnp.where(lane == 105, p_mid, jnp.where(lane == 106, p_lo, 0.0)))
    rider = jnp.where(first_row, rider, 0.0)

    def ride(i, carry):
        G[i] = (G[i].astype(F32) + rider).astype(BF16)
        return carry

    lax.fori_loop(0, ne, ride, 0)

    def a2(d):
        t = lax.rem(e + d, ne)
        b, r = place(e)
        return to(G.at[t], GF.at[2 + b, pl.ds(r, 16)], a2s.at[d], a2r.at[d], (t, g))

    @pl.loop(1, ne)
    def _(d):
        a2(d).start()

    GF[2 + b_own, pl.ds(r_own, 16), :] = G[e]

    second_far()

    def a2_in(d):
        b, r = place(lax.rem(e - d + ne, ne))
        return to(G.at[0], GF.at[2 + b, pl.ds(r, 16)], a2s.at[d], a2r.at[d], (e, g))

    @pl.loop(1, ne)
    def _(d):
        a2_in(d).wait_recv()

    g_far = [to(GF.at[2], GF.at[1], gs.at[0], gr.at[0], (e, far)), to(GF.at[3], GF.at[0], gs.at[1], gr.at[1], (e, far))]
    g_near = [to(GF.at[3], GF.at[4], gs.at[2], gr.at[2], (e, near)), to(GF.at[2], GF.at[5], gs.at[3], gr.at[3], (e, near))]

    @pl.when(has_far)
    def _():
        for c in g_far:
            c.start()

    for c in g_near:
        c.start()

    mine = GF[2:4].reshape(256, 128).astype(F32)
    lane = lax.broadcasted_iota(jnp.int32, (256, 128), 1)
    mine = jnp.where((lane >= 104) & (lane < 107), mine, 0.0)
    band = jnp.sum(jnp.sum(mine, axis=0, keepdims=True), axis=1, keepdims=True)
    LS[g] = jnp.broadcast_to(band, (8, 128))

    def tell(d):
        return to(LS.at[g], LS.at[g], ts.at[d], tr.at[d], (e, lax.rem(g + d, ng)))

    def told(d):
        s = lax.rem(g - d + ng, ng)
        return to(LS.at[s], LS.at[s], ts.at[d], tr.at[d], (e, g))

    @pl.loop(1, ng)
    def _(d):
        tell(d).start()

    pair_of = lax.broadcasted_iota(jnp.int32, (16, 1024), 0)
    pair_of = 2 * lax.rem(pair_of, 8) + pair_of // 8
    indicator = jnp.where(lax.broadcasted_iota(jnp.int32, (16, 1024), 1) // 64 == pair_of, 1.0, 0.0).astype(BF16)

    def d_mix(slot, count, own):
        rows = GF[slot : slot + count].reshape(count * 128, 128)
        twice = jnp.concatenate([rows, rows], axis=1)
        c = jnp.zeros((16, 256), F32)
        for j in range(4):
            r = nn(twice, MW[:, span(j, 256)]).astype(BF16)
            for h in range(2):
                for i in range(count):
                    DD[2 * j + h, slot + i] = stacked(r[i * 128 : (i + 1) * 128, h * 128 : (h + 1) * 128])
            if own:
                prod = r.astype(F32) * MIXF[:, :, span(j, 256)].reshape(256, 256)
                hi = prod.astype(BF16)
                lower = (prod - hi.astype(F32)).astype(BF16)
                c = c + nt(indicator[:, span(j, 256)], hi) + nt(indicator[:, span(j, 256)], lower)
        if own:
            for i in range(2):
                C[i] = jnp.concatenate([c[0:8, span(i, 128)], c[8:16, span(i, 128)]], axis=1)

    d_mix(2, 2, True)
    c_far = to(C, CR.at[0], cs.at[0], cr.at[0], (e, far))
    c_near = to(C, CR.at[1], cs.at[1], cr.at[1], (e, near))

    @pl.when(has_far)
    def _():
        c_far.start()

    c_near.start()

    def own_back(hp):
        row = pl.ds(hp, 1)
        dks, dvs = [], []
        for qi in range(2):
            other = [jnp.where(i == 3 - qi, 1.0, 0.0) for i in picked[qi][1:]]
            dp = nt(jnp.concatenate([V[hp, i] for i in picked[qi]], axis=0), DD[hp, 2 + qi])
            p = [E[qi, hp, i - qi].astype(F32) for i in picked[qi]]
            c = C[qi, row, :]
            ds = [p[n] * (dp[n * 128 : (n + 1) * 128] - c) for n in range(3)]
            half = [x.astype(BF16) for x in ds]
            keys = jnp.concatenate([KT[hp, i] for i in picked[qi]], axis=1)
            dq = diagonal(nn(keys, jnp.concatenate(half, axis=0))).T * 0.125
            DQ[qi, :, span(hp, 128)] = dq.astype(BF16)
            pair = [half[0], (ds[1] * other[0] + ds[2] * other[1]).astype(BF16)]
            prob = [E[qi, hp, 2], (p[1] * other[0] + p[2] * other[1]).astype(BF16)]
            if qi:
                pair, prob = pair[::-1], prob[::-1]
            dks.append(nn(jnp.concatenate(pair, axis=0), QQ[hp, 2 + qi]))
            dvs.append(nn(jnp.concatenate(prob, axis=0), DD[hp, 2 + qi]))
        DK[hp] = dks[0] + dks[1]
        DV[hp] = dvs[0] + dvs[1]

    unrolled(8, UNROLL_OWN, own_back)

    def foreign_back(side, final):
        q1, q2, k2 = sides[side]
        c1, c2 = (0, 1) if side == 0 else (1, 0)

        def head_pair(hp):
            row = pl.ds(hp, 1)
            p1 = PF[side, hp, 0:256]
            ds1 = (p1.astype(F32) * (nt(V[hp, 2:4].reshape(256, 128), DD[hp, q1]) - CR[side, c1, row, :])).astype(BF16)
            dk = DK[hp] + nn(ds1, QQ[hp, q1])
            dv = DV[hp] + nn(p1, DD[hp, q1])
            p2 = PF[side, hp, 256:384]
            ds2 = (p2.astype(F32) * (nt(V[hp, k2], DD[hp, q2]) - CR[side, c2, row, :])).astype(BF16)
            dk2 = nn(ds2, QQ[hp, q2])
            dv2 = nn(p2, DD[hp, q2])
            if side == 0:
                dk = jnp.concatenate([dk[:128] + dk2, dk[128:]], axis=0)
                dv = jnp.concatenate([dv[:128] + dv2, dv[128:]], axis=0)
            else:
                dk = jnp.concatenate([dk[:128], dk[128:] + dk2], axis=0)
                dv = jnp.concatenate([dv[:128], dv[128:] + dv2], axis=0)
            if final:
                lanes = span(hp, 128)
                DKB[:, lanes] = dk.astype(BF16)
                DVB[:, lanes] = dv.astype(BF16)
            else:
                DK[hp] = dk
                DV[hp] = dv

        unrolled(8, UNROLL_BACK, head_pair)

    for c in g_near:
        c.wait_recv()
    d_mix(4, 2, False)
    c_near.wait_recv()
    foreign_back(1, False)

    for j in range(4):
        lanes = span(j, 256)
        own_rows = GF[2:4].reshape(256, 128)
        DO[:, lanes] = nn(own_rows, MP[:, lanes]) + nt(DQ[...].reshape(256, 1024), WQ[lanes, :])

    @pl.when(has_far)
    def _():
        for c in g_far:
            c.wait_recv()

    d_mix(0, 2, False)

    @pl.when(has_far)
    def _():
        c_far.wait_recv()

    foreign_back(0, True)

    for j in range(4):
        lanes = span(j, 256)
        r = (DO[:, lanes] + nt(DKB[...], WK[lanes, :]) + nt(DVB[...], WV[lanes, :])).astype(BF16)
        out_ref[pl.ds(pl.multiple_of(core * 128, 128), 128), lanes] = r[:128]
        out_ref[pl.ds(pl.multiple_of((1 - core) * 128, 128), 128), lanes] = r[128:]

    @pl.loop(1, ng)
    def _(d):
        told(d).wait_recv()

    loss_ref[...] = jnp.sum(LS[...], axis=0)[0:1, 0:1] * (1.0 / (256 * ng * variables))

    @pl.when(has_far)
    def _():
        for c in [x_far[1], s_far] + p_far + g_far + [l_far, c_far]:
            c.wait_send()

    for c in x_near + g_near + [l_near, c_near]:
        c.wait_send()

    @pl.loop(1, ne)
    def _(d):
        a1(d).wait_send()
        a2(d).wait_send()

    @pl.loop(1, ng)
    def _(d):
        tell(d).wait_send()


def shards(x, wq, wk, wv, wo, decoder, targets, area_weight, key_blocks):
    ne, ng = lax.axis_size("ens"), lax.axis_size("grid")
    points, channels = x.shape[1:]
    variables = decoder.shape[0]
    vm = pltpu.VMEM
    dma = pltpu.SemaphoreType.DMA
    scratch = [vm((1024, 1024), BF16)] * 4 + [
        vm((128, 1024), BF16),
        vm((256, 1024), BF16),
        vm((256, 128), F32),
        vm((6, 128, 1024), BF16),
        vm((8, 768, 128), BF16),
        vm((8, 6, 128, 128), BF16),
        vm((8, 6, 128, 128), BF16),
        vm((8, 128, 768), BF16),
        vm((8, 6, 256, 128), BF16),
        vm((8, 6, 256, 128), BF16),
        vm((2, 8, 5, 128, 256), BF16),
        vm((2, 8, 128, 128), F32),
        vm((2, 3, 8, 256), F32),
        vm((2, 8, 256), F32),
        vm((2, 8, 256), F32),
        vm((4, 8, 256), F32),
        vm((4, 8, 256), F32),
        vm((2, 8, 256), F32),
        vm((128, 128), BF16),
        vm((128, 128), BF16),
        vm((128, 1024), BF16),
        vm((3, 8, 256), F32),
        vm((3, 8, 256), F32),
        vm((8, 256), F32),
        vm((8, 256), F32),
        vm((2, 128, 1024), F32),
        vm((2, 128, 1024), BF16),
        vm((2, 128, 128), F32),
        vm((2, 128, 128), BF16),
        vm((16, 16, 128), BF16),
        vm((16, 16, 128), F32),
        vm((16, 16, 128), BF16),
        vm((6, 128, 128), BF16),
        vm((2, 8, 384, 256), BF16),
        vm((256, 1024), F32),
        vm((2, 128, 1024), BF16),
        vm((8, 256, 128), F32),
        vm((8, 256, 128), F32),
        vm((256, 1024), BF16),
        vm((256, 1024), BF16),
        vm((2, 8, 256), F32),
        vm((2, 2, 8, 256), F32),
        vm((16, 8, 128), F32),
        dma((7,)),
        dma((4,)),
        dma((4,)),
        dma((16,)),
        dma((16,)),
        dma((16,)),
        dma((16,)),
        dma((4,)),
        dma((4,)),
        dma((2,)),
        dma((2,)),
        dma((3,)),
        dma((3,)),
        dma((2,)),
        dma((2,)),
        dma((16,)),
        dma((16,)),
    ]
    anywhere = pl.BlockSpec(memory_space=pl.ANY)
    in_vmem = pl.BlockSpec(memory_space=pltpu.VMEM)
    grad, loss = pl.pallas_call(
        functools.partial(kernel, ne, ng, variables),
        out_shape=(
            pltpu.VMEM((points, channels), BF16),
            jax.ShapeDtypeStruct((1, 1), F32),
        ),
        in_specs=[pl.BlockSpec(memory_space=pltpu.SMEM)] * 2 + [anywhere] * 5 + [in_vmem] * 2,
        out_specs=(in_vmem, in_vmem),
        scratch_shapes=scratch,
        compiler_params=pltpu.CompilerParams(
            collective_id=0, has_side_effects=True, vmem_limit_bytes=58 * 1024 * 1024
        ),
        name="whole",
    )(key_blocks, area_weight, x[0], wq, wk, wv, wo, decoder, targets)
    return grad[None], loss[0, 0]


def solution(mesh):
    return jax.shard_map(
        shards,
        mesh=mesh,
        in_specs=(
            P("ens", "grid", None),
            P(),
            P(),
            P(),
            P(),
            P(),
            P(None, "grid"),
            P("grid"),
            P("grid", None),
        ),
        out_specs=(P("ens", "grid", None), P()),
        check_vma=False,
    )
```

```python
import functools

import jax
import jax.numpy as jnp
from jax import lax
from jax.experimental import pallas as pl
from jax.experimental.pallas import tpu as pltpu
from jax.sharding import PartitionSpec as P

MESH = pl.DeviceIdType.MESH
SMOOTH = 0.25
BIG = 1e30
NEG = -1e30
F32 = jnp.float32
BF16 = jnp.bfloat16
UNROLL = 8
FIRST, SECOND = 4, 6
UNROLL_OWN = 8
UNROLL_BACK = 8


def nt(a, b):
    return lax.dot_general(a, b, (((1,), (1,)), ((), ())), preferred_element_type=F32)


def nn(a, b):
    return lax.dot_general(a, b, (((1,), (0,)), ((), ())), preferred_element_type=F32)


def heads_of(row):
    return jnp.concatenate(
        [
            jnp.broadcast_to(row[:, :128], (64, 128)),
            jnp.broadcast_to(row[:, 128:], (64, 128)),
        ],
        axis=0,
    )


def diagonal(pair):
    return jnp.concatenate([pair[:64, :128], pair[64:, 128:]], axis=0)


def unrolled(count, group, body):
    if group == count:
        for i in range(count):
            body(i)
    else:

        @pl.loop(0, count // group)
        def _(k):
            for i in range(group):
                body(k * group + i)


def span(i, width):
    if isinstance(i, int):
        return slice(i * width, (i + 1) * width)
    return pl.ds(pl.multiple_of(i * width, width), width)


def kernel(
    ne,
    ng,
    variables,
    kb_ref,
    area_ref,
    x_hbm,
    wq_hbm,
    wk_hbm,
    wv_hbm,
    wo_hbm,
    decoder_ref,
    targets_ref,
    out_ref,
    loss_ref,
    WQ,
    WK,
    WV,
    WO,
    MP,
    MW,
    TT,
    X,
    K,
    V,
    KT,
    VT,
    QQ,
    DD,
    E,
    ACC,
    MS,
    L,
    LSE,
    SO,
    SR,
    LB,
    PS,
    PR,
    MXF,
    LO,
    LR,
    LF,
    LFR,
    MIXF,
    MIXB,
    FX,
    FC,
    RV,
    G,
    GF,
    PF,
    DO,
    DQ,
    DK,
    DV,
    DKB,
    DVB,
    C,
    CR,
    LS,
    loc,
    xs,
    xr,
    a1s,
    a1r,
    a2s,
    a2r,
    gs,
    gr,
    ls,
    lr,
    ps,
    pr,
    cs,
    cr,
    ts,
    tr,
):
    e = lax.axis_index("ens")
    g = lax.axis_index("grid")
    core = lax.rem(g, 2)
    far = g - 1 + 2 * core
    near = g + 1 - 2 * core
    has_far = (far >= 0) & (far < ng)

    def load(src, dst, i):
        return pltpu.make_async_copy(src, dst, loc.at[i])

    lx = [
        load(x_hbm.at[pl.ds(pl.multiple_of(core * 128, 128), 128)], X.at[2], 0),
        load(x_hbm.at[pl.ds(pl.multiple_of((1 - core) * 128, 128), 128)], X.at[3], 1),
    ]
    lk, lv, lq = load(wk_hbm, WK, 2), load(wv_hbm, WV, 3), load(wq_hbm, WQ, 4)
    lo = load(wo_hbm, WO, 5)
    for c in lx + [lk, lv, lq, lo]:
        c.start()

    barrier = pltpu.get_barrier_semaphore()

    @pl.loop(1, ne)
    def _(d):
        pl.semaphore_signal(barrier, inc=1, device_id=(lax.rem(e + d, ne), g), device_id_type=MESH)

    @pl.loop(1, ng)
    def _(d):
        pl.semaphore_signal(barrier, inc=1, device_id=(e, lax.rem(g + d, ng)), device_id_type=MESH)

    @pl.when(jnp.logical_not(has_far))
    def _():
        X[0:2] = jnp.zeros((2, 128, 1024), BF16)
        GF[0:2] = jnp.zeros((2, 128, 128), BF16)
        LFR[...] = jnp.full((8, 256), BIG, F32)
        SR[0] = jnp.zeros((8, 256), F32)
        SR[1] = jnp.full((8, 256), BIG, F32)
        PR[...] = jnp.zeros((128, 128), BF16)
        CR[0] = jnp.zeros((2, 8, 256), F32)

    for c in lx:
        c.wait()
    pl.semaphore_wait(barrier, ne - 1 + ng - 1)

    def to(src, dst, s, r, dev):
        return pltpu.make_async_remote_copy(
            src_ref=src, dst_ref=dst, send_sem=s, recv_sem=r, device_id=dev, device_id_type=MESH
        )

    x_far = to(X.at[2], X.at[1], xs.at[0], xr.at[0], (e, far))
    x_sec = [
        to(X.at[3, span(i, 16)], X.at[0, span(i, 16)], xs.at[4 + i], xr.at[4 + i], (e, far)) for i in range(8)
    ]

    def second(first, last):
        @pl.when(has_far)
        def _():
            for c in x_sec[first:last]:
                c.start()
    x_near = [to(X.at[3], X.at[4], xs.at[2], xr.at[2], (e, near)), to(X.at[2], X.at[5], xs.at[3], xr.at[3], (e, near))]

    @pl.when(has_far)
    def _():
        x_far.start()

    for c in x_near:
        c.start()

    def slot_of(block):
        return jnp.where(core == 0, block - (2 * g - 2), 2 * g + 3 - block)

    seen, picked = [], []
    for q in range(2):
        ids = [jnp.where(core == 0, slot_of(kb_ref[q, n]), slot_of(kb_ref[1 - q, n])) for n in range(3)]
        picked.append([jnp.clip(i, q, q + 4) for i in ids])
        seen.append([(ids[0] == s) | (ids[1] == s) | (ids[2] == s) for s in range(6)])

    low = lax.broadcasted_iota(jnp.int32, (1, 128), 1) < 64

    def stacked(block):
        zero = jnp.zeros_like(block)
        return jnp.concatenate([jnp.where(low, block, zero), jnp.where(low, zero, block)], axis=0)

    def rows_of(ref, slot, count):
        return ref[slot : slot + count].reshape(count * 128, 1024)

    def project_kv(slot, count, group=4):
        def tile(j):
            rows = slice(slot * 128, (slot + count) * 128)
            k = nn(rows_of(X, slot, count), WK[:, span(j, 256)]).astype(BF16)
            v = nn(rows_of(X, slot, count), WV[:, span(j, 256)]).astype(BF16)
            for h in range(2):
                part = k[:, span(h, 128)]
                K[2 * j + h, rows, :] = part
                for i in range(count):
                    KT[2 * j + h, slot + i] = part[span(i, 128)].T
                part = v[:, span(h, 128)]
                V[2 * j + h, slot : slot + count] = part.reshape(count, 128, 128)
                VT[2 * j + h, :, rows] = part.T

        unrolled(4, group, tile)

    def project_q(slot, count, group=4):
        def tile(j):
            r = (nn(rows_of(X, slot, count), WQ[:, span(j, 256)]) * 0.125).astype(BF16)
            for h in range(2):
                for i in range(count):
                    QQ[2 * j + h, slot + i] = stacked(r[i * 128 : (i + 1) * 128, h * 128 : (h + 1) * 128])

        unrolled(4, group, tile)

    def attend(qi, first, last, step, final, group=8):
        n = last - first + 1
        off = first - qi

        def head_pair(hp):
            row = pl.ds(hp, 1)
            s = nt(K[hp, first * 128 : (last + 1) * 128, :], QQ[hp, 2 + qi])
            if step:
                m_old = MS[qi, step - 1, row, :]
                m = m_old
            else:
                m = jnp.full((1, 256), NEG, F32)
            parts = [s[i * 128 : (i + 1) * 128] for i in range(n)]
            for i, part in enumerate(parts):
                m = jnp.maximum(m, jnp.where(seen[qi][first + i], jnp.max(part, axis=0, keepdims=True), NEG))
            total = jnp.zeros((1, 256), F32)
            exps = []
            for i, part in enumerate(parts):
                x = jnp.exp(part - jnp.where(seen[qi][first + i], m, BIG))
                total = total + jnp.sum(x, axis=0, keepdims=True)
                exps.append(x.astype(BF16))
            eb = jnp.concatenate(exps, axis=0) if n > 1 else exps[0]
            E[qi, hp, off : off + n] = eb.reshape(n, 128, 256)
            acc = diagonal(nn(VT[hp, :, first * 128 : (last + 1) * 128], eb))
            if step:
                alpha = jnp.exp(m_old - m)
                total = total + L[qi, row, :] * alpha
                acc = acc + ACC[qi, hp] * heads_of(alpha)
            MS[qi, step, row, :] = m
            if final:
                LSE[qi, row, :] = m + jnp.log(total)
                mix = (acc * heads_of(1.0 / total)).T
                lanes = span(hp, 128)
                MIXF[qi, :, lanes] = mix
                MIXB[qi, :, lanes] = mix.astype(BF16)
            else:
                L[qi, row, :] = total
                ACC[qi, hp] = acc

        unrolled(8, group, head_pair)

    def decode(qi):
        f = nt(MIXB[qi], MW[...])
        FC[qi] = (FX[qi] + (f[:, :128] + f[:, 128:])).astype(BF16)

    def place(t):
        half = t // 8
        return jnp.where(core == 0, half, 1 - half), pl.multiple_of(lax.rem(t, 8) * 16, 16)

    def a1(d):
        t = lax.rem(e + d, ne)
        b, r = place(t)
        return to(FC.at[b, pl.ds(r, 16)], RV.at[e], a1s.at[d], a1r.at[d], (t, g))

    lk.wait()
    lv.wait()
    project_kv(2, 2)
    lq.wait()
    project_q(2, 2)
    for c in x_near:
        c.wait_recv()
    project_kv(4, 2)
    attend(0, 2, 4, 0, False)
    SO[0] = MS[0, 0] + jnp.log(L[0])
    SO[1, 0:4] = jnp.full((4, 256), jnp.where(seen[0][1], 0.0, BIG), F32)
    SO[1, 4:8] = jnp.full((4, 256), jnp.where(seen[0][0], 0.0, BIG), F32)
    s_far = to(SO, SR, ps.at[0], pr.at[0], (e, far))

    @pl.when(has_far)
    def _():
        s_far.start()

    attend(1, 2, 5, 0, False)
    project_q(4, 2)
    MP[...] = jnp.concatenate([decoder_ref[...], jnp.zeros((28, 1024), BF16)], axis=0)
    TT[...] = jnp.concatenate([targets_ref[...], jnp.zeros((28, 256), F32)], axis=0).T
    lo.wait()

    for j in range(4):
        r = nt(MP[...], WO[span(j, 256), :])
        hi = r.astype(BF16)
        MW[0:128, span(j, 256)] = hi
        MW[128:256, span(j, 256)] = (r - hi.astype(F32)).astype(BF16)

    for qi in range(2):
        FX[qi] = nt(X[2 + qi], MP[...])

    @pl.when(has_far)
    def _():
        x_far.wait_send()
        for c in x_sec[:FIRST]:
            c.start()
        x_far.wait_recv()
        s_far.wait_recv()

    def far_query(hp):
        row = pl.ds(hp, 1)
        s = nt(K[hp, 256:512, :], QQ[hp, 1])
        m_old, bias_a, bias_b = SR[0, row, :], SR[1, 0:1, :], SR[1, 4:5, :]
        m = jnp.maximum(m_old, jnp.max(s[:128], axis=0, keepdims=True) - bias_a)
        m = jnp.maximum(m, jnp.max(s[128:], axis=0, keepdims=True) - bias_b)
        xa, xb = jnp.exp(s[:128] - (m + bias_a)), jnp.exp(s[128:] - (m + bias_b))
        total = jnp.exp(m_old - m)
        total = total + jnp.sum(xa, axis=0, keepdims=True) + jnp.sum(xb, axis=0, keepdims=True)
        LB[0, row, :] = m + jnp.log(total)
        p = (jnp.concatenate([xa, xb], axis=0) * (1.0 / total)).astype(BF16)
        PF[0, hp, 0:256] = p
        MXF[:, span(hp, 128)] = diagonal(nn(VT[hp, :, 256:512], p)).T.astype(BF16)

    project_q(1, 1, 4)
    unrolled(8, UNROLL, far_query)
    f = nt(MXF[...], MW[...])
    PS[...] = (f[:, :128] + f[:, 128:]).astype(BF16)
    p_far = [to(PS, PR, ps.at[1], pr.at[1], (e, far)), to(LB.at[0], LB.at[1], ps.at[2], pr.at[2], (e, far))]

    @pl.when(has_far)
    def _():
        for c in p_far:
            c.start()

    @pl.when(jnp.logical_not(has_far))
    def _():
        LB[1] = MS[0, 0] + jnp.log(L[0])

    second(FIRST, SECOND)

    project_kv(1, 1, 4)
    attend(1, 1, 1, 1, True, UNROLL)
    decode(1)

    def a1_half(near_block):
        half = jnp.where(near_block, 1 - core, core)

        @pl.loop(0, 8)
        def _(i):
            t = half * 8 + i

            @pl.when(t != e)
            def _():
                a1(lax.rem(t - e + ne, ne)).start()

    a1_half(True)

    def normalise(qi, hp, spans):
        row = pl.ds(hp, 1)
        lse = LSE[qi, row, :]
        for step, (first, last) in enumerate(spans):
            scale = jnp.exp(MS[qi, step, row, :] - lse)
            a, b = first - qi, last + 1 - qi
            E[qi, hp, a:b] = (E[qi, hp, a:b].astype(F32) * scale).astype(BF16)

    unrolled(8, 4, lambda hp: normalise(1, hp, ((2, 5), (1, 1))))

    @pl.when(has_far)
    def _():
        for c in p_far:
            c.wait_recv()

    LSE[0] = LB[1]

    def far_block(hp):
        row = pl.ds(hp, 1)
        mix = (ACC[0, hp] * heads_of(jnp.exp(MS[0, 0, row, :] - LSE[0, row, :]))).T
        MIXF[0, :, span(hp, 128)] = mix
        MIXB[0, :, span(hp, 128)] = mix.astype(BF16)

    unrolled(8, 8, far_block)
    f = nt(MIXB[0], MW[...])
    FC[0] = (FX[0] + (f[:, :128] + f[:, 128:]) + PR[...].astype(F32)).astype(BF16)
    a1_half(False)

    b_own, r_own = place(e)
    RV[e] = FC[b_own, pl.ds(r_own, 16), :]

    def shown(qi, s):
        return jnp.where(seen[qi][s], LSE[qi], BIG)

    LF[...] = shown(1, 1)
    LO[0], LO[1], LO[2] = shown(1, 5), shown(1, 4), shown(0, 4)
    l_far = to(LF, LFR, ls.at[0], lr.at[0], (e, far))
    l_near = to(LO, LR, ls.at[1], lr.at[1], (e, near))

    @pl.when(has_far)
    def _():
        l_far.start()

    l_near.start()
    second(SECOND, 8)

    unrolled(8, 4, lambda hp: normalise(0, hp, ((2, 4),)))

    l_near.wait_recv()

    def near_query(hp):
        row = pl.ds(hp, 1)
        s1 = nt(K[hp, 256:512, :], QQ[hp, 4])
        PF[1, hp, 0:128] = jnp.exp(s1[:128] - LR[0, row, :]).astype(BF16)
        PF[1, hp, 128:256] = jnp.exp(s1[128:] - LR[1, row, :]).astype(BF16)
        s2 = nt(K[hp, 384:512, :], QQ[hp, 5])
        PF[1, hp, 256:384] = jnp.exp(s2 - LR[2, row, :]).astype(BF16)

    unrolled(8, 8, near_query)

    def second_far():
        @pl.when(has_far)
        def _():
            for c in x_sec:
                c.wait_recv()
            l_far.wait_recv()

        project_kv(0, 1)
        project_q(0, 1)

        def head_pair(hp):
            row = pl.ds(hp, 1)
            lse = LSE[0, row, :]
            s = nt(K[hp, 0:256, :], QQ[hp, 2])
            pa = jnp.exp(s[:128] - jnp.where(seen[0][0], lse, BIG))
            pb = jnp.exp(s[128:] - jnp.where(seen[0][1], lse, BIG))
            p = jnp.concatenate([pa, pb], axis=0).astype(BF16)
            E[0, hp, 0:2] = p.reshape(2, 128, 256)
            lanes = span(hp, 128)
            MIXF[0, :, lanes] = MIXF[0, :, lanes] + diagonal(nn(VT[hp, :, 0:256], p)).T
            s2 = nt(K[hp, 256:384, :], QQ[hp, 0])
            PF[0, hp, 256:384] = jnp.exp(s2 - LFR[row, :]).astype(BF16)

        unrolled(8, 8, head_pair)

    sides = ((1, 0, 2), (4, 5, 3))

    @pl.loop(1, ne)
    def _(d):
        a1(d).wait_recv()

    truth = TT[pl.ds(pl.multiple_of(e * 16, 16), 16), :]
    line = lax.broadcasted_iota(jnp.int32, (16, 128), 0)
    lane = lax.broadcasted_iota(jnp.int32, (16, 128), 1)
    weight = jnp.zeros((16, 128), F32)
    for i in range(16):
        weight = jnp.where(line == i, area_ref[e * 16 + i], weight)
    weight = jnp.where(lane < variables, weight, 0.0)
    members = [RV[i].astype(F32) for i in range(ne)]
    halves, total = [], jnp.zeros((8, 128), F32)
    for half in (slice(0, 8), slice(8, 16)):
        y = [x[half] for x in members]
        pulls = [jnp.zeros((8, 128), F32) for _ in range(ne)]
        pairs = jnp.zeros((8, 128), F32)
        for i in range(ne):
            for j in range(i + 1, ne):
                d = y[i] - y[j]
                v = d * d + SMOOTH * SMOOTH
                r = lax.rsqrt(v)
                u = d * r
                pulls[i] = pulls[i] + u
                pulls[j] = pulls[j] - u
                pairs = pairs + v * r
        score = (2.0 * pairs + ne * SMOOTH) * (-0.5 / (ne - 1))
        grads = []
        for i in range(ne):
            d = y[i] - truth[half]
            v = d * d + SMOOTH * SMOOTH
            r = lax.rsqrt(v)
            score = score + v * r
            grads.append(weight[half] * (d * r - pulls[i] * (1.0 / (ne - 1))))
        total = total + weight[half] * score
        halves.append(grads)
    partial = jnp.sum(jnp.sum(total, axis=0, keepdims=True), axis=1, keepdims=True)
    p_hi = partial.astype(BF16).astype(F32)
    p_mid = (partial - p_hi).astype(BF16).astype(F32)
    p_lo = partial - p_hi - p_mid
    rider = jnp.where(lane == 104, p_hi, jnp.where(lane == 105, p_mid, jnp.where(lane == 106, p_lo, 0.0)))
    rider = jnp.where(line == 0, rider, 0.0)
    for i in range(ne):
        G[i] = (jnp.concatenate([halves[0][i], halves[1][i]], axis=0) + rider).astype(BF16)

    def a2(d):
        t = lax.rem(e + d, ne)
        b, r = place(e)
        return to(G.at[t], GF.at[2 + b, pl.ds(r, 16)], a2s.at[d], a2r.at[d], (t, g))

    @pl.loop(1, ne)
    def _(d):
        a2(d).start()

    GF[2 + b_own, pl.ds(r_own, 16), :] = G[e]

    second_far()

    def a2_in(d):
        b, r = place(lax.rem(e - d + ne, ne))
        return to(G.at[0], GF.at[2 + b, pl.ds(r, 16)], a2s.at[d], a2r.at[d], (e, g))

    @pl.loop(1, ne)
    def _(d):
        a2_in(d).wait_recv()

    g_far = [to(GF.at[2], GF.at[1], gs.at[0], gr.at[0], (e, far)), to(GF.at[3], GF.at[0], gs.at[1], gr.at[1], (e, far))]
    g_near = [to(GF.at[3], GF.at[4], gs.at[2], gr.at[2], (e, near)), to(GF.at[2], GF.at[5], gs.at[3], gr.at[3], (e, near))]

    @pl.when(has_far)
    def _():
        for c in g_far:
            c.start()

    for c in g_near:
        c.start()

    mine = GF[2:4].reshape(256, 128).astype(F32)
    lane = lax.broadcasted_iota(jnp.int32, (256, 128), 1)
    mine = jnp.where((lane >= 104) & (lane < 107), mine, 0.0)
    band = jnp.sum(jnp.sum(mine, axis=0, keepdims=True), axis=1, keepdims=True)
    LS[g] = jnp.broadcast_to(band, (8, 128))

    def tell(d):
        return to(LS.at[g], LS.at[g], ts.at[d], tr.at[d], (e, lax.rem(g + d, ng)))

    def told(d):
        s = lax.rem(g - d + ng, ng)
        return to(LS.at[s], LS.at[s], ts.at[d], tr.at[d], (e, g))

    @pl.loop(1, ng)
    def _(d):
        tell(d).start()

    pair_of = lax.broadcasted_iota(jnp.int32, (16, 1024), 0)
    pair_of = 2 * lax.rem(pair_of, 8) + pair_of // 8
    indicator = jnp.where(lax.broadcasted_iota(jnp.int32, (16, 1024), 1) // 64 == pair_of, 1.0, 0.0).astype(BF16)

    def d_mix(slot, count, own):
        rows = GF[slot : slot + count].reshape(count * 128, 128)
        twice = jnp.concatenate([rows, rows], axis=1)
        c = jnp.zeros((16, 256), F32)
        for j in range(4):
            r = nn(twice, MW[:, span(j, 256)]).astype(BF16)
            for h in range(2):
                for i in range(count):
                    DD[2 * j + h, slot + i] = stacked(r[i * 128 : (i + 1) * 128, h * 128 : (h + 1) * 128])
            if own:
                prod = r.astype(F32) * MIXF[:, :, span(j, 256)].reshape(256, 256)
                hi = prod.astype(BF16)
                lower = (prod - hi.astype(F32)).astype(BF16)
                c = c + nt(indicator[:, span(j, 256)], hi) + nt(indicator[:, span(j, 256)], lower)
        if own:
            for i in range(2):
                C[i] = jnp.concatenate([c[0:8, span(i, 128)], c[8:16, span(i, 128)]], axis=1)

    d_mix(2, 2, True)
    c_far = to(C, CR.at[0], cs.at[0], cr.at[0], (e, far))
    c_near = to(C, CR.at[1], cs.at[1], cr.at[1], (e, near))

    @pl.when(has_far)
    def _():
        c_far.start()

    c_near.start()

    def own_back(hp):
        row = pl.ds(hp, 1)
        dks, dvs = [], []
        for qi in range(2):
            other = [jnp.where(i == 3 - qi, 1.0, 0.0) for i in picked[qi][1:]]
            dp = nt(jnp.concatenate([V[hp, i] for i in picked[qi]], axis=0), DD[hp, 2 + qi])
            p = [E[qi, hp, i - qi].astype(F32) for i in picked[qi]]
            c = C[qi, row, :]
            ds = [p[n] * (dp[n * 128 : (n + 1) * 128] - c) for n in range(3)]
            half = [x.astype(BF16) for x in ds]
            keys = jnp.concatenate([KT[hp, i] for i in picked[qi]], axis=1)
            dq = diagonal(nn(keys, jnp.concatenate(half, axis=0))).T * 0.125
            DQ[qi, :, span(hp, 128)] = dq.astype(BF16)
            pair = [half[0], (ds[1] * other[0] + ds[2] * other[1]).astype(BF16)]
            prob = [E[qi, hp, 2], (p[1] * other[0] + p[2] * other[1]).astype(BF16)]
            if qi:
                pair, prob = pair[::-1], prob[::-1]
            dks.append(nn(jnp.concatenate(pair, axis=0), QQ[hp, 2 + qi]))
            dvs.append(nn(jnp.concatenate(prob, axis=0), DD[hp, 2 + qi]))
        DK[hp] = dks[0] + dks[1]
        DV[hp] = dvs[0] + dvs[1]

    unrolled(8, UNROLL_OWN, own_back)

    def foreign_back(side, final):
        q1, q2, k2 = sides[side]
        c1, c2 = (0, 1) if side == 0 else (1, 0)

        def head_pair(hp):
            row = pl.ds(hp, 1)
            p1 = PF[side, hp, 0:256]
            ds1 = (p1.astype(F32) * (nt(V[hp, 2:4].reshape(256, 128), DD[hp, q1]) - CR[side, c1, row, :])).astype(BF16)
            dk = DK[hp] + nn(ds1, QQ[hp, q1])
            dv = DV[hp] + nn(p1, DD[hp, q1])
            p2 = PF[side, hp, 256:384]
            ds2 = (p2.astype(F32) * (nt(V[hp, k2], DD[hp, q2]) - CR[side, c2, row, :])).astype(BF16)
            dk2 = nn(ds2, QQ[hp, q2])
            dv2 = nn(p2, DD[hp, q2])
            if side == 0:
                dk = jnp.concatenate([dk[:128] + dk2, dk[128:]], axis=0)
                dv = jnp.concatenate([dv[:128] + dv2, dv[128:]], axis=0)
            else:
                dk = jnp.concatenate([dk[:128], dk[128:] + dk2], axis=0)
                dv = jnp.concatenate([dv[:128], dv[128:] + dv2], axis=0)
            if final:
                lanes = span(hp, 128)
                DKB[:, lanes] = dk.astype(BF16)
                DVB[:, lanes] = dv.astype(BF16)
            else:
                DK[hp] = dk
                DV[hp] = dv

        unrolled(8, UNROLL_BACK, head_pair)

    for c in g_near:
        c.wait_recv()
    d_mix(4, 2, False)
    c_near.wait_recv()
    foreign_back(1, False)

    for j in range(4):
        lanes = span(j, 256)
        own_rows = GF[2:4].reshape(256, 128)
        DO[:, lanes] = nn(own_rows, MP[:, lanes]) + nt(DQ[...].reshape(256, 1024), WQ[lanes, :])

    @pl.when(has_far)
    def _():
        for c in g_far:
            c.wait_recv()

    d_mix(0, 2, False)

    @pl.when(has_far)
    def _():
        c_far.wait_recv()

    foreign_back(0, True)

    for j in range(4):
        lanes = span(j, 256)
        r = (DO[:, lanes] + nt(DKB[...], WK[lanes, :]) + nt(DVB[...], WV[lanes, :])).astype(BF16)
        out_ref[pl.ds(pl.multiple_of(core * 128, 128), 128), lanes] = r[:128]
        out_ref[pl.ds(pl.multiple_of((1 - core) * 128, 128), 128), lanes] = r[128:]

    @pl.loop(1, ng)
    def _(d):
        told(d).wait_recv()

    loss_ref[...] = jnp.sum(LS[...], axis=0)[0:1, 0:1] * (1.0 / (256 * ng * variables))

    @pl.when(has_far)
    def _():
        for c in x_sec + [s_far] + p_far + g_far + [l_far, c_far]:
            c.wait_send()

    for c in x_near + g_near + [l_near, c_near]:
        c.wait_send()

    @pl.loop(1, ne)
    def _(d):
        a1(d).wait_send()
        a2(d).wait_send()

    @pl.loop(1, ng)
    def _(d):
        tell(d).wait_send()


def shards(x, wq, wk, wv, wo, decoder, targets, area_weight, key_blocks):
    ne, ng = lax.axis_size("ens"), lax.axis_size("grid")
    points, channels = x.shape[1:]
    variables = decoder.shape[0]
    vm = pltpu.VMEM
    dma = pltpu.SemaphoreType.DMA
    scratch = [vm((1024, 1024), BF16)] * 4 + [
        vm((128, 1024), BF16),
        vm((256, 1024), BF16),
        vm((256, 128), F32),
        vm((6, 128, 1024), BF16),
        vm((8, 768, 128), BF16),
        vm((8, 6, 128, 128), BF16),
        vm((8, 6, 128, 128), BF16),
        vm((8, 128, 768), BF16),
        vm((8, 6, 256, 128), BF16),
        vm((8, 6, 256, 128), BF16),
        vm((2, 8, 5, 128, 256), BF16),
        vm((2, 8, 128, 128), F32),
        vm((2, 3, 8, 256), F32),
        vm((2, 8, 256), F32),
        vm((2, 8, 256), F32),
        vm((2, 8, 256), F32),
        vm((2, 8, 256), F32),
        vm((2, 8, 256), F32),
        vm((128, 128), BF16),
        vm((128, 128), BF16),
        vm((128, 1024), BF16),
        vm((3, 8, 256), F32),
        vm((3, 8, 256), F32),
        vm((8, 256), F32),
        vm((8, 256), F32),
        vm((2, 128, 1024), F32),
        vm((2, 128, 1024), BF16),
        vm((2, 128, 128), F32),
        vm((2, 128, 128), BF16),
        vm((16, 16, 128), BF16),
        vm((16, 16, 128), BF16),
        vm((6, 128, 128), BF16),
        vm((2, 8, 384, 256), BF16),
        vm((256, 1024), F32),
        vm((2, 128, 1024), BF16),
        vm((8, 256, 128), F32),
        vm((8, 256, 128), F32),
        vm((256, 1024), BF16),
        vm((256, 1024), BF16),
        vm((2, 8, 256), F32),
        vm((2, 2, 8, 256), F32),
        vm((16, 8, 128), F32),
        dma((7,)),
        dma((12,)),
        dma((12,)),
        dma((16,)),
        dma((16,)),
        dma((16,)),
        dma((16,)),
        dma((4,)),
        dma((4,)),
        dma((2,)),
        dma((2,)),
        dma((3,)),
        dma((3,)),
        dma((2,)),
        dma((2,)),
        dma((16,)),
        dma((16,)),
    ]
    anywhere = pl.BlockSpec(memory_space=pl.ANY)
    in_vmem = pl.BlockSpec(memory_space=pltpu.VMEM)
    grad, loss = pl.pallas_call(
        functools.partial(kernel, ne, ng, variables),
        out_shape=(
            pltpu.VMEM((points, channels), BF16),
            jax.ShapeDtypeStruct((1, 1), F32),
        ),
        in_specs=[pl.BlockSpec(memory_space=pltpu.SMEM)] * 2 + [anywhere] * 5 + [in_vmem] * 2,
        out_specs=(in_vmem, in_vmem),
        scratch_shapes=scratch,
        compiler_params=pltpu.CompilerParams(
            collective_id=0, has_side_effects=True, vmem_limit_bytes=58 * 1024 * 1024
        ),
        name="whole",
    )(key_blocks, area_weight, x[0], wq, wk, wv, wo, decoder, targets)
    return grad[None], loss[0, 0]


def solution(mesh):
    return jax.shard_map(
        shards,
        mesh=mesh,
        in_specs=(
            P("ens", "grid", None),
            P(),
            P(),
            P(),
            P(),
            P(),
            P(None, "grid"),
            P("grid"),
            P("grid", None),
        ),
        out_specs=(P("ens", "grid", None), P()),
        check_vma=False,
    )
```

```python
import functools

import jax
import jax.numpy as jnp
from jax import lax
from jax.experimental import pallas as pl
from jax.experimental.pallas import tpu as pltpu
from jax.sharding import PartitionSpec as P

MESH = pl.DeviceIdType.MESH
SMOOTH = 0.25
BIG = 1e30
NEG = -1e30
F32 = jnp.float32
BF16 = jnp.bfloat16
UNROLL = 8
FIRST, SECOND = 4, 6
UNROLL_OWN = 8
UNROLL_BACK = 8


def nt(a, b):
    return lax.dot_general(a, b, (((1,), (1,)), ((), ())), preferred_element_type=F32)


def nn(a, b):
    return lax.dot_general(a, b, (((1,), (0,)), ((), ())), preferred_element_type=F32)


def heads_of(row):
    return jnp.concatenate(
        [
            jnp.broadcast_to(row[:, :128], (64, 128)),
            jnp.broadcast_to(row[:, 128:], (64, 128)),
        ],
        axis=0,
    )


def diagonal(pair):
    return jnp.concatenate([pair[:64, :128], pair[64:, 128:]], axis=0)


def unrolled(count, group, body):
    if group == count:
        for i in range(count):
            body(i)
    else:

        @pl.loop(0, count // group)
        def _(k):
            for i in range(group):
                body(k * group + i)


def span(i, width):
    if isinstance(i, int):
        return slice(i * width, (i + 1) * width)
    return pl.ds(pl.multiple_of(i * width, width), width)


def kernel(
    ne,
    ng,
    variables,
    kb_ref,
    area_ref,
    x_hbm,
    wq_hbm,
    wk_hbm,
    wv_hbm,
    wo_hbm,
    decoder_ref,
    targets_ref,
    out_ref,
    loss_ref,
    WQ,
    WK,
    WV,
    WO,
    MP,
    MW,
    TT,
    X,
    K,
    V,
    KT,
    VT,
    QQ,
    DD,
    E,
    ACC,
    MS,
    L,
    LSE,
    SO,
    SR,
    LB,
    PS,
    PR,
    MXF,
    LO,
    LR,
    LF,
    LFR,
    MIXF,
    MIXB,
    FX,
    FC,
    RV,
    G,
    GF,
    PF,
    DO,
    DQ,
    DK,
    DV,
    DKB,
    DVB,
    C,
    CR,
    LS,
    loc,
    xs,
    xr,
    a1s,
    a1r,
    a2s,
    a2r,
    gs,
    gr,
    ls,
    lr,
    ps,
    pr,
    cs,
    cr,
    ts,
    tr,
):
    e = lax.axis_index("ens")
    g = lax.axis_index("grid")
    core = lax.rem(g, 2)
    far = g - 1 + 2 * core
    near = g + 1 - 2 * core
    has_far = (far >= 0) & (far < ng)

    def load(src, dst, i):
        return pltpu.make_async_copy(src, dst, loc.at[i])

    lx = [
        load(x_hbm.at[pl.ds(pl.multiple_of(core * 128, 128), 128)], X.at[2], 0),
        load(x_hbm.at[pl.ds(pl.multiple_of((1 - core) * 128, 128), 128)], X.at[3], 1),
    ]
    lk, lv, lq = load(wk_hbm, WK, 2), load(wv_hbm, WV, 3), load(wq_hbm, WQ, 4)
    lo = load(wo_hbm, WO, 5)
    for c in lx + [lk, lv, lq, lo]:
        c.start()

    barrier = pltpu.get_barrier_semaphore()

    @pl.loop(1, ne)
    def _(d):
        pl.semaphore_signal(barrier, inc=1, device_id=(lax.rem(e + d, ne), g), device_id_type=MESH)

    @pl.loop(1, ng)
    def _(d):
        pl.semaphore_signal(barrier, inc=1, device_id=(e, lax.rem(g + d, ng)), device_id_type=MESH)

    @pl.when(jnp.logical_not(has_far))
    def _():
        X[0:2] = jnp.zeros((2, 128, 1024), BF16)
        GF[0:2] = jnp.zeros((2, 128, 128), BF16)
        LFR[...] = jnp.full((8, 256), BIG, F32)
        SR[0] = jnp.zeros((8, 256), F32)
        SR[1] = jnp.full((8, 256), BIG, F32)
        PR[...] = jnp.zeros((128, 128), BF16)
        CR[0] = jnp.zeros((2, 8, 256), F32)

    for c in lx:
        c.wait()
    pl.semaphore_wait(barrier, ne - 1 + ng - 1)

    def to(src, dst, s, r, dev):
        return pltpu.make_async_remote_copy(
            src_ref=src, dst_ref=dst, send_sem=s, recv_sem=r, device_id=dev, device_id_type=MESH
        )

    x_far = to(X.at[2], X.at[1], xs.at[0], xr.at[0], (e, far))
    x_sec = [
        to(X.at[3, span(i, 16)], X.at[0, span(i, 16)], xs.at[4 + i], xr.at[4 + i], (e, far)) for i in range(8)
    ]

    def second(first, last):
        @pl.when(has_far)
        def _():
            for c in x_sec[first:last]:
                c.start()
    x_near = [to(X.at[3], X.at[4], xs.at[2], xr.at[2], (e, near)), to(X.at[2], X.at[5], xs.at[3], xr.at[3], (e, near))]

    @pl.when(has_far)
    def _():
        x_far.start()

    for c in x_near:
        c.start()

    def slot_of(block):
        return jnp.where(core == 0, block - (2 * g - 2), 2 * g + 3 - block)

    seen, picked = [], []
    for q in range(2):
        ids = [jnp.where(core == 0, slot_of(kb_ref[q, n]), slot_of(kb_ref[1 - q, n])) for n in range(3)]
        picked.append([jnp.clip(i, q, q + 4) for i in ids])
        seen.append([(ids[0] == s) | (ids[1] == s) | (ids[2] == s) for s in range(6)])

    low = lax.broadcasted_iota(jnp.int32, (1, 128), 1) < 64

    def stacked(block):
        zero = jnp.zeros_like(block)
        return jnp.concatenate([jnp.where(low, block, zero), jnp.where(low, zero, block)], axis=0)

    def rows_of(ref, slot, count):
        return ref[slot : slot + count].reshape(count * 128, 1024)

    def project_kv(slot, count, group=4):
        def tile(j):
            rows = slice(slot * 128, (slot + count) * 128)
            k = nn(rows_of(X, slot, count), WK[:, span(j, 256)]).astype(BF16)
            v = nn(rows_of(X, slot, count), WV[:, span(j, 256)]).astype(BF16)
            for h in range(2):
                part = k[:, span(h, 128)]
                K[2 * j + h, rows, :] = part
                for i in range(count):
                    KT[2 * j + h, slot + i] = part[span(i, 128)].T
                part = v[:, span(h, 128)]
                V[2 * j + h, slot : slot + count] = part.reshape(count, 128, 128)
                VT[2 * j + h, :, rows] = part.T

        unrolled(4, group, tile)

    def project_q(slot, count, group=4):
        def tile(j):
            r = (nn(rows_of(X, slot, count), WQ[:, span(j, 256)]) * 0.125).astype(BF16)
            for h in range(2):
                for i in range(count):
                    QQ[2 * j + h, slot + i] = stacked(r[i * 128 : (i + 1) * 128, h * 128 : (h + 1) * 128])

        unrolled(4, group, tile)

    def attend(qi, first, last, step, final, group=8):
        n = last - first + 1
        off = first - qi

        def head_pair(hp):
            row = pl.ds(hp, 1)
            s = nt(K[hp, first * 128 : (last + 1) * 128, :], QQ[hp, 2 + qi])
            if step:
                m_old = MS[qi, step - 1, row, :]
                m = m_old
            else:
                m = jnp.full((1, 256), NEG, F32)
            parts = [s[i * 128 : (i + 1) * 128] for i in range(n)]
            for i, part in enumerate(parts):
                m = jnp.maximum(m, jnp.where(seen[qi][first + i], jnp.max(part, axis=0, keepdims=True), NEG))
            total = jnp.zeros((1, 256), F32)
            exps = []
            for i, part in enumerate(parts):
                x = jnp.exp(part - jnp.where(seen[qi][first + i], m, BIG))
                total = total + jnp.sum(x, axis=0, keepdims=True)
                exps.append(x.astype(BF16))
            eb = jnp.concatenate(exps, axis=0) if n > 1 else exps[0]
            E[qi, hp, off : off + n] = eb.reshape(n, 128, 256)
            acc = diagonal(nn(VT[hp, :, first * 128 : (last + 1) * 128], eb))
            if step:
                alpha = jnp.exp(m_old - m)
                total = total + L[qi, row, :] * alpha
                acc = acc + ACC[qi, hp] * heads_of(alpha)
            MS[qi, step, row, :] = m
            if final:
                LSE[qi, row, :] = m + jnp.log(total)
                mix = (acc * heads_of(1.0 / total)).T
                lanes = span(hp, 128)
                MIXF[qi, :, lanes] = mix
                MIXB[qi, :, lanes] = mix.astype(BF16)
            else:
                L[qi, row, :] = total
                ACC[qi, hp] = acc

        unrolled(8, group, head_pair)

    def decode(qi):
        f = nt(MIXB[qi], MW[...])
        FC[qi] = (FX[qi] + (f[:, :128] + f[:, 128:])).astype(BF16)

    def place(t):
        half = t // 8
        return jnp.where(core == 0, half, 1 - half), pl.multiple_of(lax.rem(t, 8) * 16, 16)

    def a1(d):
        t = lax.rem(e + d, ne)
        b, r = place(t)
        return to(FC.at[b, pl.ds(r, 16)], RV.at[e], a1s.at[d], a1r.at[d], (t, g))

    lk.wait()
    lv.wait()
    project_kv(2, 2)
    lq.wait()
    project_q(2, 2)
    for c in x_near:
        c.wait_recv()
    project_kv(4, 2)
    attend(0, 2, 4, 0, False)
    SO[0] = MS[0, 0] + jnp.log(L[0])
    SO[1, 0:4] = jnp.full((4, 256), jnp.where(seen[0][1], 0.0, BIG), F32)
    SO[1, 4:8] = jnp.full((4, 256), jnp.where(seen[0][0], 0.0, BIG), F32)
    s_far = to(SO, SR, ps.at[0], pr.at[0], (e, far))

    @pl.when(has_far)
    def _():
        s_far.start()

    attend(1, 2, 5, 0, False)
    project_q(4, 2)
    MP[...] = jnp.concatenate([decoder_ref[...], jnp.zeros((28, 1024), BF16)], axis=0)
    TT[...] = jnp.concatenate([targets_ref[...], jnp.zeros((28, 256), F32)], axis=0).T
    lo.wait()

    for j in range(4):
        r = nt(MP[...], WO[span(j, 256), :])
        hi = r.astype(BF16)
        MW[0:128, span(j, 256)] = hi
        MW[128:256, span(j, 256)] = (r - hi.astype(F32)).astype(BF16)

    for qi in range(2):
        FX[qi] = nt(X[2 + qi], MP[...])

    @pl.when(has_far)
    def _():
        x_far.wait_send()
        for c in x_sec[:FIRST]:
            c.start()
        x_far.wait_recv()
        s_far.wait_recv()

    def far_query(hp):
        row = pl.ds(hp, 1)
        s = nt(K[hp, 256:512, :], QQ[hp, 1])
        m_old, bias_a, bias_b = SR[0, row, :], SR[1, 0:1, :], SR[1, 4:5, :]
        m = jnp.maximum(m_old, jnp.max(s[:128], axis=0, keepdims=True) - bias_a)
        m = jnp.maximum(m, jnp.max(s[128:], axis=0, keepdims=True) - bias_b)
        xa, xb = jnp.exp(s[:128] - (m + bias_a)), jnp.exp(s[128:] - (m + bias_b))
        total = jnp.exp(m_old - m)
        total = total + jnp.sum(xa, axis=0, keepdims=True) + jnp.sum(xb, axis=0, keepdims=True)
        LB[0, row, :] = m + jnp.log(total)
        p = (jnp.concatenate([xa, xb], axis=0) * (1.0 / total)).astype(BF16)
        PF[0, hp, 0:256] = p
        MXF[:, span(hp, 128)] = diagonal(nn(VT[hp, :, 256:512], p)).T.astype(BF16)

    project_q(1, 1, 4)
    unrolled(8, UNROLL, far_query)
    p_far = [to(PS, PR, ps.at[1], pr.at[1], (e, far)), to(LB.at[0], LB.at[1], ps.at[2], pr.at[2], (e, far))]

    @pl.when(has_far)
    def _():
        p_far[1].start()

    f = nt(MXF[...], MW[...])
    PS[...] = (f[:, :128] + f[:, 128:]).astype(BF16)

    @pl.when(has_far)
    def _():
        p_far[0].start()

    @pl.when(jnp.logical_not(has_far))
    def _():
        LB[1] = MS[0, 0] + jnp.log(L[0])

    second(FIRST, SECOND)

    project_kv(1, 1, 4)
    attend(1, 1, 1, 1, True, UNROLL)
    decode(1)

    def a1_half(near_block):
        half = jnp.where(near_block, 1 - core, core)

        @pl.loop(0, 8)
        def _(i):
            t = half * 8 + i

            @pl.when(t != e)
            def _():
                a1(lax.rem(t - e + ne, ne)).start()

    a1_half(True)

    def normalise(qi, hp, spans):
        row = pl.ds(hp, 1)
        lse = LSE[qi, row, :]
        for step, (first, last) in enumerate(spans):
            scale = jnp.exp(MS[qi, step, row, :] - lse)
            a, b = first - qi, last + 1 - qi
            E[qi, hp, a:b] = (E[qi, hp, a:b].astype(F32) * scale).astype(BF16)

    unrolled(8, 4, lambda hp: normalise(1, hp, ((2, 5), (1, 1))))

    @pl.when(has_far)
    def _():
        for c in p_far:
            c.wait_recv()

    LSE[0] = LB[1]

    def far_block(hp):
        row = pl.ds(hp, 1)
        mix = (ACC[0, hp] * heads_of(jnp.exp(MS[0, 0, row, :] - LSE[0, row, :]))).T
        MIXF[0, :, span(hp, 128)] = mix
        MIXB[0, :, span(hp, 128)] = mix.astype(BF16)

    unrolled(8, 8, far_block)
    f = nt(MIXB[0], MW[...])
    FC[0] = (FX[0] + (f[:, :128] + f[:, 128:]) + PR[...].astype(F32)).astype(BF16)
    a1_half(False)

    b_own, r_own = place(e)
    RV[e] = FC[b_own, pl.ds(r_own, 16), :]

    def shown(qi, s):
        return jnp.where(seen[qi][s], LSE[qi], BIG)

    LF[...] = shown(1, 1)
    LO[0], LO[1], LO[2] = shown(1, 5), shown(1, 4), shown(0, 4)
    l_far = to(LF, LFR, ls.at[0], lr.at[0], (e, far))
    l_near = to(LO, LR, ls.at[1], lr.at[1], (e, near))

    @pl.when(has_far)
    def _():
        l_far.start()

    l_near.start()
    second(SECOND, 8)

    unrolled(8, 4, lambda hp: normalise(0, hp, ((2, 4),)))

    l_near.wait_recv()

    def near_query(hp):
        row = pl.ds(hp, 1)
        s1 = nt(K[hp, 256:512, :], QQ[hp, 4])
        PF[1, hp, 0:128] = jnp.exp(s1[:128] - LR[0, row, :]).astype(BF16)
        PF[1, hp, 128:256] = jnp.exp(s1[128:] - LR[1, row, :]).astype(BF16)
        s2 = nt(K[hp, 384:512, :], QQ[hp, 5])
        PF[1, hp, 256:384] = jnp.exp(s2 - LR[2, row, :]).astype(BF16)

    unrolled(8, 8, near_query)

    def second_far():
        @pl.when(has_far)
        def _():
            for c in x_sec:
                c.wait_recv()
            l_far.wait_recv()

        project_kv(0, 1)
        project_q(0, 1)

        def head_pair(hp):
            row = pl.ds(hp, 1)
            lse = LSE[0, row, :]
            s = nt(K[hp, 0:256, :], QQ[hp, 2])
            pa = jnp.exp(s[:128] - jnp.where(seen[0][0], lse, BIG))
            pb = jnp.exp(s[128:] - jnp.where(seen[0][1], lse, BIG))
            p = jnp.concatenate([pa, pb], axis=0).astype(BF16)
            E[0, hp, 0:2] = p.reshape(2, 128, 256)
            lanes = span(hp, 128)
            MIXF[0, :, lanes] = MIXF[0, :, lanes] + diagonal(nn(VT[hp, :, 0:256], p)).T
            s2 = nt(K[hp, 256:384, :], QQ[hp, 0])
            PF[0, hp, 256:384] = jnp.exp(s2 - LFR[row, :]).astype(BF16)

        unrolled(8, 8, head_pair)

    sides = ((1, 0, 2), (4, 5, 3))

    @pl.loop(1, ne)
    def _(d):
        a1(d).wait_recv()

    truth = TT[pl.ds(pl.multiple_of(e * 16, 16), 16), :]
    line = lax.broadcasted_iota(jnp.int32, (16, 128), 0)
    lane = lax.broadcasted_iota(jnp.int32, (16, 128), 1)
    weight = jnp.zeros((16, 128), F32)
    for i in range(16):
        weight = jnp.where(line == i, area_ref[e * 16 + i], weight)
    weight = jnp.where(lane < variables, weight, 0.0)
    members = [RV[i].astype(F32) for i in range(ne)]
    halves, total = [], jnp.zeros((8, 128), F32)
    for half in (slice(0, 8), slice(8, 16)):
        y = [x[half] for x in members]
        pulls = [jnp.zeros((8, 128), F32) for _ in range(ne)]
        pairs = jnp.zeros((8, 128), F32)
        for i in range(ne):
            for j in range(i + 1, ne):
                d = y[i] - y[j]
                v = d * d + SMOOTH * SMOOTH
                r = lax.rsqrt(v)
                u = d * r
                pulls[i] = pulls[i] + u
                pulls[j] = pulls[j] - u
                pairs = pairs + v * r
        score = (2.0 * pairs + ne * SMOOTH) * (-0.5 / (ne - 1))
        grads = []
        for i in range(ne):
            d = y[i] - truth[half]
            v = d * d + SMOOTH * SMOOTH
            r = lax.rsqrt(v)
            score = score + v * r
            grads.append(weight[half] * (d * r - pulls[i] * (1.0 / (ne - 1))))
        total = total + weight[half] * score
        halves.append(grads)
    partial = jnp.sum(jnp.sum(total, axis=0, keepdims=True), axis=1, keepdims=True)
    p_hi = partial.astype(BF16).astype(F32)
    p_mid = (partial - p_hi).astype(BF16).astype(F32)
    p_lo = partial - p_hi - p_mid
    rider = jnp.where(lane == 104, p_hi, jnp.where(lane == 105, p_mid, jnp.where(lane == 106, p_lo, 0.0)))
    rider = jnp.where(line == 0, rider, 0.0)
    for i in range(ne):
        G[i] = (jnp.concatenate([halves[0][i], halves[1][i]], axis=0) + rider).astype(BF16)

    def a2(d):
        t = lax.rem(e + d, ne)
        b, r = place(e)
        return to(G.at[t], GF.at[2 + b, pl.ds(r, 16)], a2s.at[d], a2r.at[d], (t, g))

    @pl.loop(1, ne)
    def _(d):
        a2(d).start()

    GF[2 + b_own, pl.ds(r_own, 16), :] = G[e]

    second_far()

    def a2_in(d):
        b, r = place(lax.rem(e - d + ne, ne))
        return to(G.at[0], GF.at[2 + b, pl.ds(r, 16)], a2s.at[d], a2r.at[d], (e, g))

    @pl.loop(1, ne)
    def _(d):
        a2_in(d).wait_recv()

    g_far = [to(GF.at[2], GF.at[1], gs.at[0], gr.at[0], (e, far)), to(GF.at[3], GF.at[0], gs.at[1], gr.at[1], (e, far))]
    g_near = [to(GF.at[3], GF.at[4], gs.at[2], gr.at[2], (e, near)), to(GF.at[2], GF.at[5], gs.at[3], gr.at[3], (e, near))]

    @pl.when(has_far)
    def _():
        for c in g_far:
            c.start()

    for c in g_near:
        c.start()

    pair_of = lax.broadcasted_iota(jnp.int32, (16, 1024), 0)
    pair_of = 2 * lax.rem(pair_of, 8) + pair_of // 8
    indicator = jnp.where(lax.broadcasted_iota(jnp.int32, (16, 1024), 1) // 64 == pair_of, 1.0, 0.0).astype(BF16)

    def d_mix(slot, count, own):
        rows = GF[slot : slot + count].reshape(count * 128, 128)
        twice = jnp.concatenate([rows, rows], axis=1)
        c = jnp.zeros((16, 256), F32)
        for j in range(4):
            r = nn(twice, MW[:, span(j, 256)]).astype(BF16)
            for h in range(2):
                for i in range(count):
                    DD[2 * j + h, slot + i] = stacked(r[i * 128 : (i + 1) * 128, h * 128 : (h + 1) * 128])
            if own:
                prod = r.astype(F32) * MIXF[:, :, span(j, 256)].reshape(256, 256)
                hi = prod.astype(BF16)
                lower = (prod - hi.astype(F32)).astype(BF16)
                c = c + nt(indicator[:, span(j, 256)], hi) + nt(indicator[:, span(j, 256)], lower)
        if own:
            for i in range(2):
                C[i] = jnp.concatenate([c[0:8, span(i, 128)], c[8:16, span(i, 128)]], axis=1)

    d_mix(2, 2, True)
    c_far = to(C, CR.at[0], cs.at[0], cr.at[0], (e, far))
    c_near = to(C, CR.at[1], cs.at[1], cr.at[1], (e, near))

    @pl.when(has_far)
    def _():
        c_far.start()

    c_near.start()

    mine = GF[2:4].reshape(256, 128).astype(F32)
    lane = lax.broadcasted_iota(jnp.int32, (256, 128), 1)
    mine = jnp.where((lane >= 104) & (lane < 107), mine, 0.0)
    band = jnp.sum(jnp.sum(mine, axis=0, keepdims=True), axis=1, keepdims=True)
    LS[g] = jnp.broadcast_to(band, (8, 128))

    def tell(d):
        return to(LS.at[g], LS.at[g], ts.at[d], tr.at[d], (e, lax.rem(g + d, ng)))

    def told(d):
        s = lax.rem(g - d + ng, ng)
        return to(LS.at[s], LS.at[s], ts.at[d], tr.at[d], (e, g))

    @pl.loop(1, ng)
    def _(d):
        tell(d).start()

    def own_back(hp):
        row = pl.ds(hp, 1)
        dks, dvs = [], []
        for qi in range(2):
            other = [jnp.where(i == 3 - qi, 1.0, 0.0) for i in picked[qi][1:]]
            dp = nt(jnp.concatenate([V[hp, i] for i in picked[qi]], axis=0), DD[hp, 2 + qi])
            p = [E[qi, hp, i - qi].astype(F32) for i in picked[qi]]
            c = C[qi, row, :]
            ds = [p[n] * (dp[n * 128 : (n + 1) * 128] - c) for n in range(3)]
            half = [x.astype(BF16) for x in ds]
            keys = jnp.concatenate([KT[hp, i] for i in picked[qi]], axis=1)
            dq = diagonal(nn(keys, jnp.concatenate(half, axis=0))).T * 0.125
            DQ[qi, :, span(hp, 128)] = dq.astype(BF16)
            pair = [half[0], (ds[1] * other[0] + ds[2] * other[1]).astype(BF16)]
            prob = [E[qi, hp, 2], (p[1] * other[0] + p[2] * other[1]).astype(BF16)]
            if qi:
                pair, prob = pair[::-1], prob[::-1]
            dks.append(nn(jnp.concatenate(pair, axis=0), QQ[hp, 2 + qi]))
            dvs.append(nn(jnp.concatenate(prob, axis=0), DD[hp, 2 + qi]))
        DK[hp] = dks[0] + dks[1]
        DV[hp] = dvs[0] + dvs[1]

    unrolled(8, UNROLL_OWN, own_back)

    def foreign_back(side, final):
        q1, q2, k2 = sides[side]
        c1, c2 = (0, 1) if side == 0 else (1, 0)

        def head_pair(hp):
            row = pl.ds(hp, 1)
            p1 = PF[side, hp, 0:256]
            ds1 = (p1.astype(F32) * (nt(V[hp, 2:4].reshape(256, 128), DD[hp, q1]) - CR[side, c1, row, :])).astype(BF16)
            dk = DK[hp] + nn(ds1, QQ[hp, q1])
            dv = DV[hp] + nn(p1, DD[hp, q1])
            p2 = PF[side, hp, 256:384]
            ds2 = (p2.astype(F32) * (nt(V[hp, k2], DD[hp, q2]) - CR[side, c2, row, :])).astype(BF16)
            dk2 = nn(ds2, QQ[hp, q2])
            dv2 = nn(p2, DD[hp, q2])
            if side == 0:
                dk = jnp.concatenate([dk[:128] + dk2, dk[128:]], axis=0)
                dv = jnp.concatenate([dv[:128] + dv2, dv[128:]], axis=0)
            else:
                dk = jnp.concatenate([dk[:128], dk[128:] + dk2], axis=0)
                dv = jnp.concatenate([dv[:128], dv[128:] + dv2], axis=0)
            if final:
                lanes = span(hp, 128)
                DKB[:, lanes] = dk.astype(BF16)
                DVB[:, lanes] = dv.astype(BF16)
            else:
                DK[hp] = dk
                DV[hp] = dv

        unrolled(8, UNROLL_BACK, head_pair)

    for c in g_near:
        c.wait_recv()
    d_mix(4, 2, False)
    c_near.wait_recv()
    foreign_back(1, False)

    for j in range(4):
        lanes = span(j, 256)
        own_rows = GF[2:4].reshape(256, 128)
        DO[:, lanes] = nn(own_rows, MP[:, lanes]) + nt(DQ[...].reshape(256, 1024), WQ[lanes, :])

    @pl.when(has_far)
    def _():
        for c in g_far:
            c.wait_recv()

    d_mix(0, 2, False)

    @pl.when(has_far)
    def _():
        c_far.wait_recv()

    foreign_back(0, True)

    for j in range(4):
        lanes = span(j, 256)
        r = (DO[:, lanes] + nt(DKB[...], WK[lanes, :]) + nt(DVB[...], WV[lanes, :])).astype(BF16)
        out_ref[pl.ds(pl.multiple_of(core * 128, 128), 128), lanes] = r[:128]
        out_ref[pl.ds(pl.multiple_of((1 - core) * 128, 128), 128), lanes] = r[128:]

    @pl.loop(1, ng)
    def _(d):
        told(d).wait_recv()

    loss_ref[...] = jnp.sum(LS[...], axis=0)[0:1, 0:1] * (1.0 / (256 * ng * variables))

    @pl.when(has_far)
    def _():
        for c in x_sec + [s_far] + p_far + g_far + [l_far, c_far]:
            c.wait_send()

    for c in x_near + g_near + [l_near, c_near]:
        c.wait_send()

    @pl.loop(1, ne)
    def _(d):
        a1(d).wait_send()
        a2(d).wait_send()

    @pl.loop(1, ng)
    def _(d):
        tell(d).wait_send()


def shards(x, wq, wk, wv, wo, decoder, targets, area_weight, key_blocks):
    ne, ng = lax.axis_size("ens"), lax.axis_size("grid")
    points, channels = x.shape[1:]
    variables = decoder.shape[0]
    vm = pltpu.VMEM
    dma = pltpu.SemaphoreType.DMA
    scratch = [vm((1024, 1024), BF16)] * 4 + [
        vm((128, 1024), BF16),
        vm((256, 1024), BF16),
        vm((256, 128), F32),
        vm((6, 128, 1024), BF16),
        vm((8, 768, 128), BF16),
        vm((8, 6, 128, 128), BF16),
        vm((8, 6, 128, 128), BF16),
        vm((8, 128, 768), BF16),
        vm((8, 6, 256, 128), BF16),
        vm((8, 6, 256, 128), BF16),
        vm((2, 8, 5, 128, 256), BF16),
        vm((2, 8, 128, 128), F32),
        vm((2, 3, 8, 256), F32),
        vm((2, 8, 256), F32),
        vm((2, 8, 256), F32),
        vm((2, 8, 256), F32),
        vm((2, 8, 256), F32),
        vm((2, 8, 256), F32),
        vm((128, 128), BF16),
        vm((128, 128), BF16),
        vm((128, 1024), BF16),
        vm((3, 8, 256), F32),
        vm((3, 8, 256), F32),
        vm((8, 256), F32),
        vm((8, 256), F32),
        vm((2, 128, 1024), F32),
        vm((2, 128, 1024), BF16),
        vm((2, 128, 128), F32),
        vm((2, 128, 128), BF16),
        vm((16, 16, 128), BF16),
        vm((16, 16, 128), BF16),
        vm((6, 128, 128), BF16),
        vm((2, 8, 384, 256), BF16),
        vm((256, 1024), F32),
        vm((2, 128, 1024), BF16),
        vm((8, 256, 128), F32),
        vm((8, 256, 128), F32),
        vm((256, 1024), BF16),
        vm((256, 1024), BF16),
        vm((2, 8, 256), F32),
        vm((2, 2, 8, 256), F32),
        vm((16, 8, 128), F32),
        dma((7,)),
        dma((12,)),
        dma((12,)),
        dma((16,)),
        dma((16,)),
        dma((16,)),
        dma((16,)),
        dma((4,)),
        dma((4,)),
        dma((2,)),
        dma((2,)),
        dma((3,)),
        dma((3,)),
        dma((2,)),
        dma((2,)),
        dma((16,)),
        dma((16,)),
    ]
    anywhere = pl.BlockSpec(memory_space=pl.ANY)
    in_vmem = pl.BlockSpec(memory_space=pltpu.VMEM)
    grad, loss = pl.pallas_call(
        functools.partial(kernel, ne, ng, variables),
        out_shape=(
            pltpu.VMEM((points, channels), BF16),
            jax.ShapeDtypeStruct((1, 1), F32),
        ),
        in_specs=[pl.BlockSpec(memory_space=pltpu.SMEM)] * 2 + [anywhere] * 5 + [in_vmem] * 2,
        out_specs=(in_vmem, in_vmem),
        scratch_shapes=scratch,
        compiler_params=pltpu.CompilerParams(
            collective_id=0, has_side_effects=True, vmem_limit_bytes=58 * 1024 * 1024
        ),
        name="whole",
    )(key_blocks, area_weight, x[0], wq, wk, wv, wo, decoder, targets)
    return grad[None], loss[0, 0]


def solution(mesh):
    return jax.shard_map(
        shards,
        mesh=mesh,
        in_specs=(
            P("ens", "grid", None),
            P(),
            P(),
            P(),
            P(),
            P(),
            P(None, "grid"),
            P("grid"),
            P("grid", None),
        ),
        out_specs=(P("ens", "grid", None), P()),
        check_vma=False,
    )
```
